256 devices in a mesh: grp: 16 (over z, x_hi), blk: 16 (over x_lo, y, core).
Axes of the slice: x: 4 (x_hi: 2, x_lo: 2; x = x_hi * 2 + x_lo), y: 4, z: 8, core: 2. Of those that a mesh axis runs over, the one named last changes fastest.
Arguments:
- image_emb: bfloat16 [98304, 1152], P(('grp', 'blk')), may hold values from -6 to 6
- text_emb: bfloat16 [98304, 1152], P(('grp', 'blk')), may hold values from -6 to 6
- labels: int32 [98304], P(('grp', 'blk')), may hold values from 0 to 98303, as said below
- logit_params: float32 [2], replicated, may hold values from -2 to 0.05, as said below
Outputs:
- grad_image: float32 [98304, 1152], P(('grp', 'blk'))
- grad_text: float32 [98304, 1152], P(('grp', 'blk'))
- row_stats: float32 [3, 98304], P(None, ('grp', 'blk'))
The draws below stay inside these ranges and needn't reach their ends.
Inputs may be any that keep to these rules, and one draw needn't show every extreme that they name: `labels`: the positive text row of an image row of block p lies in a block of the window W(p). `logit_params`: entry 0 is the logit scale, entry 1 the logit bias.
All inputs are finite; a program needn't handle non-finite values.
Results may differ from the reference program's by a relative error of at most 0.0024.
Values may be sent and summed in bfloat16 or wider, within the bound.
No kernel may reach another device: no remote copies, remote signals or barrier semaphores. Data moves between devices by JAX's collectives and lax.ppermute only.
A program may use at most 64 MiB of HBM per device.

```python
import jax
import jax.numpy as jnp
from jax import lax

D = 1152
ROWS_DEV = 384
STEPS = 4
ROUNDS = 2
GROUPS = 16
CYCLE = 16
TOKENS = 98304


def draw_labels(key, part):
    key = jax.random.fold_in(key, 11)
    key_round, key_step, key_row = jax.random.split(key, 3)
    rows = jnp.arange(TOKENS, dtype=jnp.int32)
    block = rows // ROWS_DEV
    group = block // CYCLE
    place = block % CYCLE
    rnd = jax.random.randint(key_round, (TOKENS,), 0, ROUNDS, dtype=jnp.int32)
    step = jax.random.randint(key_step, (TOKENS,), 0, STEPS, dtype=jnp.int32)
    offset = jax.random.randint(key_row, (TOKENS,), 0, ROWS_DEV, dtype=jnp.int32)
    target = (group - rnd) % GROUPS * CYCLE + (place - step) % CYCLE
    return target * ROWS_DEV + offset


def draw_logit_params(key, part):
    key = jax.random.fold_in(key, 7)
    key_scale, key_bias = jax.random.split(key)
    scale = jnp.exp(jax.random.uniform(key_scale, (1,), jnp.float32, jnp.log(0.02), jnp.log(0.05)))
    bias = jax.random.uniform(key_bias, (1,), jnp.float32, -2.0, 0.0)
    return jnp.concatenate([scale, bias]).astype(jnp.float32)


def block_levels(own_key, dims, pieces, low, largest):
    gain = 1.0
    for dim, parts in pieces:
        heights = jax.random.uniform(jax.random.fold_in(jax.random.fold_in(own_key, 6), dim), (parts,), jnp.float32, low / len(pieces), largest / len(pieces))
        gain = gain * jnp.repeat(jnp.exp(heights), dims[dim] // parts).reshape((-1,) + (1,) * (len(dims) - 1 - dim))
    return gain


def gaussian(key, dims, deviation, reach, cuts=(), kind=jnp.bfloat16):
    loudness = block_levels(key, dims, cuts, -0.22, 0.18) if cuts else 1.0
    result = jax.random.normal(key, dims, jnp.float32) * deviation * loudness
    return jnp.minimum(jnp.maximum(result, -reach), reach).astype(kind)


def setup_inputs(seed: int = 0) -> dict:
    splits = jax.random.split(jax.random.key(seed), 5)
    return {
        "image_emb": gaussian(splits[0], (TOKENS, D), 1.0, 6.0, ((0, 256),)),
        "text_emb": gaussian(splits[1], (TOKENS, D), 1.0, 6.0, ((0, 256),)),
        "labels": draw_labels(jax.random.fold_in(splits[4], 71), 0),
        "logit_params": draw_logit_params(jax.random.fold_in(splits[4], 71), 0),
    }


def pair_tile(image, text, labels, base, scale, bias):
    raw = jnp.dot(image, text.T, preferred_element_type=jnp.float32)
    logits = scale * raw + bias
    column = base + jnp.arange(text.shape[0], dtype=jnp.int32)
    positive = (labels[:, None] == column[None, :]).astype(jnp.float32)
    sign_value = 2.0 * positive - 1.0
    loss_value = jax.nn.softplus(-sign_value * logits)
    gradient = jax.nn.sigmoid(logits) - positive
    grad_low = gradient.astype(jnp.bfloat16)
    grad_rows = jnp.dot(grad_low, text, preferred_element_type=jnp.float32)
    grad_cols = jnp.dot(grad_low.T, image, preferred_element_type=jnp.float32)
    summary = jnp.stack([jnp.sum(loss_value, axis=1), jnp.sum(gradient, axis=1), jnp.sum(gradient * raw, axis=1)])
    return grad_rows, grad_cols, summary


def reference(image_emb, text_emb, labels, logit_params):
    scale = logit_params[0]
    bias = logit_params[1]
    blocks = GROUPS * CYCLE

    def one_block(index, carry):
        grad_img, grad_txt, stats = carry
        index = jnp.asarray(index).astype(jnp.int32)
        start = (index * ROWS_DEV).astype(jnp.int32)
        image = lax.dynamic_slice_in_dim(image_emb, start, ROWS_DEV, 0)
        label_rows = lax.dynamic_slice_in_dim(labels, start, ROWS_DEV, 0)
        group = index // CYCLE
        place = index % CYCLE
        total_rows = jnp.zeros((ROWS_DEV, D), jnp.float32)
        total_stats = jnp.zeros((3, ROWS_DEV), jnp.float32)
        for rnd in range(ROUNDS):
            for step in range(STEPS):
                target = (((group - rnd) % GROUPS) * CYCLE + (place - step) % CYCLE).astype(jnp.int32)
                tstart = (target * ROWS_DEV).astype(jnp.int32)
                text = lax.dynamic_slice_in_dim(text_emb, tstart, ROWS_DEV, 0)
                rows_part, cols_part, summary = pair_tile(image, text, label_rows, tstart, scale, bias)
                total_rows = total_rows + rows_part
                total_stats = total_stats + summary
                older = lax.dynamic_slice_in_dim(grad_txt, tstart, ROWS_DEV, 0)
                grad_txt = lax.dynamic_update_slice_in_dim(grad_txt, older + cols_part, tstart, 0)
        grad_img = lax.dynamic_update_slice_in_dim(grad_img, scale * total_rows, start, 0)
        stats = lax.dynamic_update_slice(stats, total_stats, (jnp.int32(0), start))
        return grad_img, grad_txt, stats

    init = (jnp.zeros((TOKENS, D), jnp.float32), jnp.zeros((TOKENS, D), jnp.float32), jnp.zeros((3, TOKENS), jnp.float32))
    grad_img, grad_txt, stats = lax.fori_loop(0, blocks, one_block, init)
    return grad_img, scale * grad_txt, stats
```

```python
import functools

import jax
import jax.numpy as jnp
from jax import lax
from jax.experimental import pallas as pl
from jax.experimental.pallas import tpu as pltpu
from jax.sharding import PartitionSpec as P

STEPS = 4
ROUNDS = 2
AXES = ("grp", "blk")
TAIL = 16


def dot_nt(a, b):
    return lax.dot_general(a, b, (((1,), (1,)), ((), ())), preferred_element_type=jnp.float32)


def dot_nn(a, b):
    return lax.dot_general(a, b, (((1,), (0,)), ((), ())), preferred_element_type=jnp.float32)


def dot_tn(a, b):
    return lax.dot_general(a, b, (((0,), (0,)), ((), ())), preferred_element_type=jnp.float32)


def tile(par, text, image_ref, base, want_stats):
    n = text.shape[0]
    scale, bias = par[0], par[1]
    raw = dot_nt(text, image_ref[0:n, :])
    z = scale * raw + bias
    codes = image_ref[n : n + TAIL, 0:n].astype(jnp.float32)
    rel = codes[0:1, :] * 64.0 + codes[1:2, :]
    row = (lax.broadcasted_iota(jnp.int32, raw.shape, 0) + base).astype(jnp.float32)
    pos = rel == row
    e = jnp.exp(-jnp.abs(z))
    sig = jnp.where(z >= 0.0, 1.0, e) / (1.0 + e)
    grad = sig - jnp.where(pos, 1.0, 0.0)
    low = grad.astype(jnp.bfloat16)
    if not want_stats:
        return low, None
    loss = jnp.maximum(jnp.where(pos, -z, z), 0.0) + jnp.log1p(e)
    sums = jnp.concatenate(
        [
            jnp.sum(loss, axis=0, keepdims=True),
            jnp.sum(grad, axis=0, keepdims=True),
            jnp.sum(grad * raw, axis=0, keepdims=True),
        ],
        axis=0,
    )
    return low, sums


def k_own(par, idx, image, text, extra, gi, gt, st):
    n = text.shape[0]
    low, sums = tile(par, text[...], image, 0, True)
    gt[...] = dot_nn(low, image[0:n, :])
    gi[...] = dot_tn(low, text[...])
    st[0:3, :] = sums

    @pl.when(idx[1] > 0)
    def _():
        low, sums = tile(par, extra[...], image, idx[2], True)
        gi[...] += dot_tn(low, extra[...])
        st[0:3, :] += sums


def k_both(par, idx, image, other_text, text, other_image, gi0, gt0, st0, gi, gt, st, *, at_text, at_image):
    n = text.shape[0]
    low, sums = tile(par, other_text[...], image, idx[at_text], True)
    gi[...] = gi0[...] + dot_tn(low, other_text[...])
    st[0:3, :] = st0[0:3, :] + sums
    low, _ = tile(par, text[...], other_image, idx[at_image], False)
    gt[...] = gt0[...] + dot_nn(low, other_image[0:n, :])


def k_text(par, idx, text, other_image, gt0, gt, *, at_image):
    n = text.shape[0]
    low, _ = tile(par, text[...], other_image, idx[at_image], False)
    gt[...] = gt0[...] + dot_nn(low, other_image[0:n, :])


def k_cross(par, idx, text, im0, im1, im2, im3, out, acc):
    n = text.shape[0]
    far = ROUNDS // 2 * STEPS * n
    for q, (im, at) in enumerate(((im0, 0), (im1, 3), (im2, 5), (im3, 4))):
        low, _ = tile(par, text[...], im, far + idx[at], False)
        part = dot_nn(low, im[0:n, :])
        if q == 0:
            acc[...] = part
        elif q < 3:
            acc[...] += part
        else:
            out[...] = (acc[...] + part).astype(jnp.bfloat16)


def k_away(par, idx, image, text_a, text_b, out):
    n = text_a.shape[0]
    far = STEPS * n

    @pl.when(idx[6] > 0)
    def _():
        low_a, sums_a = tile(par, text_a[...], image, 3 * n, True)
        low_b, sums_b = tile(par, text_b[...], image, far + 3 * n, True)
        part = dot_tn(low_a, text_a[...]) + dot_tn(low_b, text_b[...])
        out[0:n, :] = part.astype(jnp.bfloat16)
        sums = sums_a + sums_b
        high = sums.astype(jnp.bfloat16)
        rest = (sums - high.astype(jnp.float32)).astype(jnp.bfloat16)
        last = (sums - high.astype(jnp.float32) - rest.astype(jnp.float32)).astype(jnp.bfloat16)
        fill = jnp.zeros((TAIL - 9, n), jnp.bfloat16)
        out[n : n + TAIL, :] = jnp.zeros((TAIL, out.shape[1]), jnp.bfloat16)
        out[n : n + TAIL, 0:n] = jnp.concatenate([high, rest, last, fill], axis=0)

    @pl.when(idx[6] <= 0)
    def _():
        out[...] = jnp.zeros(out.shape, jnp.bfloat16)


def k_image(par, idx, image, tx0, tx1, tx2, tx3, gi0, st0, gi, st):
    n = tx0.shape[0]
    far = STEPS * n
    low, sums = tile(par, tx0[...], image, far, True)
    gi[...] = gi0[...] + dot_tn(low, tx0[...])
    st[0:3, :] = st0[0:3, :] + sums
    for tx, at in ((tx1, 3), (tx2, 4)):
        low, sums = tile(par, tx[...], image, far + (2 * n if at == 3 else idx[7]), True)
        gi[...] += dot_tn(low, tx[...])
        st[0:3, :] += sums

    @pl.when(idx[1] > 0)
    def _():
        low, sums = tile(par, tx3[...], image, far + idx[2], True)
        gi[...] += dot_tn(low, tx3[...])
        st[0:3, :] += sums


def call(body, par, idx, ins, outs, units, alias=None, scratch=()):
    full = [pl.BlockSpec(memory_space=pltpu.SMEM)] * 2 + [pl.BlockSpec(memory_space=pltpu.VMEM)] * len(ins)
    size = sum(a.size * a.dtype.itemsize for a in ins)
    many = len(outs) > 1
    return pl.pallas_call(
        body,
        out_shape=outs if many else outs[0],
        in_specs=full,
        out_specs=[pl.BlockSpec(memory_space=pltpu.VMEM)] * len(outs)
        if many
        else pl.BlockSpec(memory_space=pltpu.VMEM),
        scratch_shapes=list(scratch),
        input_output_aliases=alias or {},
        compiler_params=pltpu.CompilerParams(vmem_limit_bytes=48 * 1024 * 1024),
        cost_estimate=pl.CostEstimate(
            flops=units * 2 * 384 * 384 * 1152, bytes_accessed=size, transcendentals=units * 384 * 384
        ),
    )(par, idx, *ins)


def on_device(image_emb, text_emb, labels, logit_params):
    n, d = image_emb.shape
    groups = lax.axis_size("grp")
    cycle = lax.axis_size("blk")
    group = lax.axis_index("grp")
    place = lax.axis_index("blk")
    core = place % 2
    half = cycle // 2
    row = place % half // 2
    hot = (row == 0) | (row == 3)

    def row_of(k):
        return k % half // 2

    def send(value, pairs):
        return lax.ppermute(value, AXES, pairs)

    def moves(dg, dk, keep=lambda k: True):
        return [
            (g * cycle + k, (g + dg) % groups * cycle + (k + dk) % cycle)
            for g in range(groups)
            for k in range(cycle)
            if keep(k)
        ]

    swap = [(g * cycle + k, g * cycle + (k ^ 1)) for g in range(groups) for k in range(cycle)]
    tie = lax.optimization_barrier

    block = labels // n
    rel = (group - block // cycle) % groups * (STEPS * n) + (place - block % cycle) % cycle * n + labels % n
    code = jnp.zeros((TAIL, d), jnp.bfloat16)
    code = code.at[0, 0:n].set((rel // 64).astype(jnp.bfloat16)).at[1, 0:n].set((rel % 64).astype(jnp.bfloat16))
    image = jnp.concatenate([image_emb, code], axis=0)

    wrap_low = row == 0
    far_first = jnp.where(core == 1, 1, 3) * n
    idx = jnp.stack(
        [
            jnp.int32(0),
            ((core == 1) | wrap_low).astype(jnp.int32),
            far_first.astype(jnp.int32),
            jnp.int32(2 * n),
            (jnp.where(core == 0, 1, 3) * n).astype(jnp.int32),
            (jnp.where(core == 0, 3, 1) * n).astype(jnp.int32),
            ((core == 1) & (row != 3)).astype(jnp.int32),
            (jnp.where(core == 0, 1, 3) * n).astype(jnp.int32),
        ]
    )
    par = logit_params
    f32 = jax.ShapeDtypeStruct((n, d), jnp.float32)
    stat = jax.ShapeDtypeStruct((8, n), jnp.float32)

    a1 = send(text_emb, moves(0, 2))
    b_cool = send(text_emb, moves(1, 0, lambda k: row_of(k) in (1, 2)))
    i1 = send(image, moves(0, -2))
    a_extra = send(
        text_emb,
        moves(0, 1, lambda k: k % 2 == 0) + moves(0, 3, lambda k: k % half == 5),
    )
    g_img, g_txt, stats = call(k_own, par, idx, [image, text_emb, a_extra], [f32, f32, stat], 5)
    a1, i1, b_cool, text, image = tie((a1, i1, b_cool, text_emb, image))

    b_hot = send(text, moves(1, 0, lambda k: row_of(k) in (0, 3)))
    b1_own = send(
        jnp.where(row == 3, text, b_cool),
        moves(0, 2, lambda k: row_of(k) in (1, 2)) + moves(1, 2, lambda k: row_of(k) == 3),
    )
    b1_over = send(a1, moves(1, 0, lambda k: row_of(k) == 1))
    a1x = send(a1, swap)
    i1x = send(i1, swap)
    g_img, g_txt, stats = call(
        functools.partial(k_both, at_text=3, at_image=3),
        par, idx, [image, a1, text, i1, g_img, g_txt, stats], [f32, f32, stat], 4, {6: 0, 7: 1, 8: 2},
    )
    a1x, i1x, i1b, g_img, g_txt = tie((a1x, i1x, i1, g_img, g_txt))
    i_last = send(jnp.where(core == 1, image, i1b), moves(0, -1, lambda k: k % half != 0))
    i_wrap = send(image, moves(0, -3, lambda k: k % half == 2))
    g_img, g_txt, stats = call(
        functools.partial(k_both, at_text=7, at_image=5),
        par, idx, [image, a1x, text, i1x, g_img, g_txt, stats], [f32, f32, stat], 4, {6: 0, 7: 1, 8: 2},
    )
    i_last = jnp.where(place % half == half - 1, i_wrap, i_last)
    g_txt = call(functools.partial(k_text, at_image=4), par, idx, [text, i_last, g_txt], [f32], 2, {4: 0})
    b_hot, b1_own, b1_over, g_txt, g_img = tie((b_hot, b1_own, b1_over, g_txt, g_img))
    b0 = jnp.where(hot, b_hot, b_cool)
    b1 = jnp.where(row == 1, b1_over, b1_own)

    cross = call(
        k_cross, par, idx, [b0, image, i1, i1x, i_last],
        [jax.ShapeDtypeStruct((n, d), jnp.bfloat16)], 8, None, [pltpu.VMEM((n, d), jnp.float32)],
    )
    back = send(cross, moves(-1, 0))
    b1x = send(b1, swap)
    b_extra = send(
        jnp.where(core == 1, text, b0),
        moves(0, 1, lambda k: k % 2 == 0) + moves(1, 3, lambda k: k % half == 5),
    )
    away = call(k_away, par, idx, [i1x, a1, b1], [jax.ShapeDtypeStruct((n + TAIL, d), jnp.bfloat16)], 4)
    home = send(away, moves(0, 1, lambda k: k % 2 == 1 and k % half != half - 1))
    g_img, stats = call(
        k_image, par, idx, [image, b0, b1, b1x, b_extra, g_img, stats], [f32, stat], 8, {7: 0, 8: 1}
    )

    scale = logit_params[0]
    home32 = home.astype(jnp.float32)
    sums = home32[n : n + 9, 0:n]
    grad_image = scale * (g_img + home32[0:n])
    row_stats = stats[0:3] + (sums[0:3] + sums[3:6] + sums[6:9])
    grad_text = scale * (g_txt + back.astype(jnp.float32))
    return grad_image, grad_text, row_stats


def solution(mesh):
    return jax.shard_map(
        on_device,
        mesh=mesh,
        in_specs=(P(AXES, None), P(AXES, None), P(AXES), P()),
        out_specs=(P(AXES, None), P(AXES, None), P(None, AXES)),
        check_vma=False,
    )
```

```python
import functools

import jax
import jax.numpy as jnp
from jax import lax
from jax.experimental import pallas as pl
from jax.experimental.pallas import tpu as pltpu
from jax.sharding import PartitionSpec as P

STEPS = 4
AXES = ("grp", "blk")
TAIL = 16


def dot_nt(a, b):
    return lax.dot_general(a, b, (((1,), (1,)), ((), ())), preferred_element_type=jnp.float32)


def dot_nn(a, b):
    return lax.dot_general(a, b, (((1,), (0,)), ((), ())), preferred_element_type=jnp.float32)


def dot_tn(a, b):
    return lax.dot_general(a, b, (((0,), (0,)), ((), ())), preferred_element_type=jnp.float32)


def spot(cycle):
    place = lax.axis_index("blk")
    return lax.rem(place, 2), lax.div(lax.rem(place, cycle // 2), 2), cycle // 4 - 1


def decode(tail, n):
    codes = tail[:, 0:n].astype(jnp.float32)
    return codes[0:1, :] * 64.0 + codes[1:2, :]


def pair(par, texts, images, rel, row, want_stats):
    scale, bias = par[0], par[1]
    raw = dot_nt(texts, images)
    z = scale * raw + bias
    pos = rel == row
    e = jnp.exp(-jnp.abs(z))
    part = 1.0 / (1.0 + e)
    sig = jnp.where(z >= 0.0, part, e * part)
    grad = jnp.where(pos, sig - 1.0, sig)
    low = grad.astype(jnp.bfloat16)
    if not want_stats:
        return low, None
    loss = jnp.maximum(jnp.where(pos, -z, z), 0.0) + jnp.log1p(e)
    sums = [jnp.sum(v, axis=0, keepdims=True) for v in (loss, grad, grad * raw)]
    return low, jnp.concatenate(sums, axis=0)


def rows(n, *bases):
    one = lax.broadcasted_iota(jnp.int32, (n, 1), 0)
    return jnp.concatenate([one + b for b in bases], axis=0).astype(jnp.float32)


def copy(source, target, sem):
    return pltpu.make_async_copy(source, target, sem)


def start(*copies):
    for c in copies:
        c.start()


def wait(*copies):
    for c in copies:
        c.wait()


def k_pack(label, image_h, text_h, full_h, other_h, out_h, image, text, code, sem, *, cycle, groups):
    core, row, _ = spot(cycle)
    n = image.shape[0]
    load_i, load_t = copy(image_h, image, sem.at[0]), copy(text_h, text, sem.at[1])
    start(load_i, load_t)
    here = label[...]
    owner = lax.div(here, n)
    rnd = lax.rem(lax.axis_index("grp") - lax.div(owner, cycle) + groups, groups)
    step = lax.rem(lax.axis_index("blk") - lax.rem(owner, cycle) + cycle, cycle)
    rel = rnd * (STEPS * n) + step * n + lax.rem(here, n)
    code[...] = jnp.zeros(code.shape, jnp.bfloat16)
    fill = jnp.zeros((TAIL - 2, n), jnp.float32)
    parts = [lax.div(rel, 64).astype(jnp.float32), lax.rem(rel, 64).astype(jnp.float32), fill]
    code[:, 0:n] = jnp.concatenate(parts, axis=0).astype(jnp.bfloat16)
    marks = [copy(code, t.at[n : n + TAIL], sem.at[q + 2]) for q, t in enumerate((full_h, other_h, out_h))]
    start(*marks)
    wait(load_i, load_t)
    whole = copy(image, full_h.at[0:n], sem.at[5])
    whole.start()

    @pl.when(core == 0)
    def _():
        copy(text, other_h.at[0:n], sem.at[6]).start()

    @pl.when(core == 1)
    def _():
        copy(image, other_h.at[0:n], sem.at[6]).start()

    @pl.when((core == 0) & (row == 1))
    def _():
        copy(image, out_h.at[0:n], sem.at[7]).start()

    @pl.when((core == 1) | (row != 1))
    def _():
        copy(text, out_h.at[0:n], sem.at[7]).start()

    wait(*marks, whole)
    copy(text, other_h.at[0:n], sem.at[6]).wait()
    copy(text, out_h.at[0:n], sem.at[7]).wait()


def k_mix(inner_h, text_h, out_h, hold, sem, *, cycle):
    _, row, last = spot(cycle)

    @pl.when(row != last)
    def _():
        copy(inner_h, hold, sem.at[0]).start()

    @pl.when(row == last)
    def _():
        copy(text_h, hold, sem.at[0]).start()

    copy(inner_h, hold, sem.at[0]).wait()
    out = copy(hold, out_h, sem.at[1])
    out.start()
    out.wait()


def k_first(par, image_h, text_h, other_h, gi_h, gt_h, st, image, tail, text, extra, etail, gi, gt, sem, *, cycle):
    core, _, _ = spot(cycle)
    n = text.shape[0]
    loads = [
        copy(image_h.at[0:n], image, sem.at[0]),
        copy(image_h.at[n : n + TAIL], tail, sem.at[1]),
        copy(text_h, text, sem.at[2]),
        copy(other_h.at[0:n], extra, sem.at[3]),
        copy(other_h.at[n : n + TAIL], etail, sem.at[4]),
    ]
    start(*loads)
    wait(*loads[0:3])
    rel = decode(tail[...], n)
    low, sums = pair(par, text[...], image[...], rel, rows(n, 0), True)
    gt[...] = dot_nn(low, image[...])
    gi[...] = dot_tn(low, text[...])
    st[0:3, :] = sums
    wait(*loads[3:])

    @pl.when(core == 1)
    def _():
        low, sums = pair(par, extra[...], image[...], rel, rows(n, n), True)
        gi[...] += dot_tn(low, extra[...])
        st[0:3, :] += sums

    @pl.when(core == 0)
    def _():
        low, _ = pair(par, text[...], extra[...], decode(etail[...], n), rows(n, n), False)
        gt[...] += dot_nn(low, extra[...])

    out = [copy(gi, gi_h, sem.at[5]), copy(gt, gt_h, sem.at[6])]
    start(*out)
    wait(*out)


def k_second(
    par, st0, image_h, text_h, t1_h, t1x_h, i1_h, i1x_h, gi0_h, gt0_h, gi_h, gt_h, st,
    image, tail, text, texts, images, tails, gi, gt, sem, *, cycle,
):
    core, row, _ = spot(cycle)
    n = text.shape[0]
    near = core == 0
    loads = [
        copy(image_h.at[0:n], image, sem.at[0]),
        copy(image_h.at[n : n + TAIL], tail, sem.at[1]),
        copy(t1_h, texts.at[0:n], sem.at[2]),
        copy(t1x_h, texts.at[n : 2 * n], sem.at[3]),
        copy(gi0_h, gi, sem.at[4]),
    ]
    more = [
        copy(text_h, text, sem.at[5]),
        copy(i1_h.at[0:n], images.at[0:n], sem.at[6]),
        copy(i1_h.at[n : n + TAIL], tails.at[0:TAIL], sem.at[7]),
        copy(i1x_h.at[0:n], images.at[n : 2 * n], sem.at[8]),
        copy(i1x_h.at[n : n + TAIL], tails.at[TAIL : 2 * TAIL], sem.at[9]),
        copy(gt0_h, gt, sem.at[10]),
    ]
    out_i = copy(gi, gi_h, sem.at[11])
    start(*loads, *more)
    wait(*loads)

    @pl.when(row > 0)
    def _():
        row_i = rows(n, 2 * n, jnp.where(near, n, 3 * n))
        low, sums = pair(par, texts[...], image[...], decode(tail[...], n), row_i, True)
        gi[...] += dot_tn(low, texts[...])
        st[0:3, :] = st0[0:3, :] + sums

    @pl.when(row == 0)
    def _():
        st[0:3, :] = st0[0:3, :]

    out_i.start()
    wait(*more)
    rel = jnp.concatenate(
        [
            decode(tails[0:TAIL, :], n) - jnp.float32(2 * n),
            decode(tails[TAIL : 2 * TAIL, :], n) - jnp.where(near, 3 * n, n).astype(jnp.float32),
        ],
        axis=1,
    )
    low, _ = pair(par, text[...], images[...], rel, rows(n, 0), False)
    gt[...] += dot_nn(low, images[...])
    out_t = copy(gt, gt_h, sem.at[12])
    out_t.start()
    wait(out_i, out_t)


def k_cross(
    par, inner_h, out_h, image_h, other_h, i1_h, i1x_h, i2_h, out, b0_h,
    text, images, tails, sem, *, cycle,
):
    core, row, last = spot(cycle)
    n = text.shape[0]
    near = core == 0

    def part(source, q):
        return (
            copy(source.at[0:n], images.at[q * n : (q + 1) * n], sem.at[2 * q]),
            copy(source.at[n : n + TAIL], tails.at[q * TAIL : (q + 1) * TAIL], sem.at[2 * q + 1]),
        )

    @pl.when(row == 0)
    def _():
        copy(out_h.at[0:n], text, sem.at[8]).start()

    @pl.when(row > 0)
    def _():
        copy(inner_h, text, sem.at[8]).start()

    for q, source in enumerate((image_h, i1_h, i1x_h)):
        start(*part(source, q))

    @pl.when(near)
    def _():
        start(*part(other_h, 3))

    @pl.when((core == 1) & (row != last))
    def _():
        start(*part(i2_h, 3))

    @pl.when((core == 1) & (row == last))
    def _():
        start(*part(out_h, 3))

    copy(inner_h, text, sem.at[8]).wait()
    keep = copy(text, b0_h, sem.at[9])
    keep.start()
    for q in range(4):
        wait(*part(image_h, q))
    steps = (0, 2 * n, jnp.where(near, 3 * n, n), jnp.where(near, n, 3 * n))
    rel = [
        decode(tails[q * TAIL : (q + 1) * TAIL, :], n) - jnp.asarray(s + STEPS * n, jnp.float32)
        for q, s in enumerate(steps)
    ]
    row_t = rows(n, 0)
    first, _ = pair(par, text[...], images[0 : 2 * n, :], jnp.concatenate(rel[0:2], axis=1), row_t, False)
    second, _ = pair(par, text[...], images[2 * n : 4 * n, :], jnp.concatenate(rel[2:4], axis=1), row_t, False)
    out[...] = dot_nn(jnp.concatenate([first, second], axis=1), images[...]).astype(jnp.bfloat16)
    keep.wait()


def k_away(par, image_h, t1_h, edge_h, over_h, mix_h, out_h, t2_h, image, tail, texts, out, sem, *, cycle):
    core, row, _ = spot(cycle)
    n = t1_h.shape[0]
    first, second = texts.at[0:n], texts.at[n : 2 * n]

    @pl.when(row == 1)
    def _():
        copy(over_h, second, sem.at[0]).start()

    @pl.when(row != 1)
    def _():
        copy(mix_h, second, sem.at[0]).start()

    @pl.when(row == 0)
    def _():
        copy(edge_h, first, sem.at[3]).start()

    @pl.when(row != 0)
    def _():
        copy(t1_h, first, sem.at[3]).start()

    loads = [copy(image_h.at[0:n], image, sem.at[1]), copy(image_h.at[n : n + TAIL], tail, sem.at[2])]
    start(*loads)
    copy(mix_h, second, sem.at[0]).wait()
    keep = copy(second, t2_h, sem.at[4])
    keep.start()
    copy(t1_h, first, sem.at[3]).wait()
    wait(*loads)

    @pl.when(core == 1)
    def _():
        row_i = rows(n, 3 * n, (STEPS + 3) * n)
        low, sums = pair(par, texts[...], image[...], decode(tail[...], n), row_i, True)
        out[0:n, :] = dot_tn(low, texts[...]).astype(jnp.bfloat16)
        high = sums.astype(jnp.bfloat16)
        rest = sums - high.astype(jnp.float32)
        mid = rest.astype(jnp.bfloat16)
        end = (rest - mid.astype(jnp.float32)).astype(jnp.bfloat16)
        fill = jnp.zeros((TAIL - 9, n), jnp.bfloat16)
        out[n : n + TAIL, :] = jnp.zeros((TAIL, out.shape[1]), jnp.bfloat16)
        out[n : n + TAIL, 0:n] = jnp.concatenate([high, mid, end, fill], axis=0)
        done = copy(out, out_h, sem.at[5])
        done.start()
        done.wait()

    keep.wait()


def k_mid(
    par, st0, b0_h, image_h, text_h, i2_h, out_h, gi0_h, gt0_h, gi_h, gt_h, st,
    b0, image, tail, text, extra, etail, gi, gt, sem, *, cycle,
):
    core, row, last = spot(cycle)
    n = text.shape[0]
    loads = [
        copy(b0_h, b0, sem.at[0]),
        copy(image_h.at[0:n], image, sem.at[1]),
        copy(image_h.at[n : n + TAIL], tail, sem.at[2]),
        copy(gi0_h, gi, sem.at[3]),
    ]
    start(*loads)

    @pl.when(core == 1)
    def _():
        start(copy(text_h, text, sem.at[5]), copy(gt0_h, gt, sem.at[6]))

    @pl.when((core == 1) & (row != last))
    def _():
        start(copy(i2_h.at[0:n], extra, sem.at[7]), copy(i2_h.at[n : n + TAIL], etail, sem.at[8]))

    @pl.when((core == 1) & (row == last))
    def _():
        start(copy(out_h.at[0:n], extra, sem.at[7]), copy(out_h.at[n : n + TAIL], etail, sem.at[8]))

    wait(*loads)
    low, sums = pair(par, b0[...], image[...], decode(tail[...], n), rows(n, STEPS * n), True)
    gi[...] += dot_tn(low, b0[...])
    st[0:3, :] = st0[0:3, :] + sums
    done = copy(gi, gi_h, sem.at[10])
    done.start()

    @pl.when(core == 1)
    def _():
        wait(copy(text_h, text, sem.at[5]), copy(gt0_h, gt, sem.at[6]))
        wait(copy(i2_h.at[0:n], extra, sem.at[7]), copy(i2_h.at[n : n + TAIL], etail, sem.at[8]))
        low, _ = pair(par, text[...], extra[...], decode(etail[...], n), rows(n, 3 * n), False)
        gt[...] += dot_nn(low, extra[...])
        copy(gt, gt_h, sem.at[9]).start()
        copy(gt, gt_h, sem.at[9]).wait()

    done.wait()


def k_late(par, st0, image_h, t2_h, bx_h, edge_h, gi0_h, gi_h, st, texts, image, tail, gi, sem, *, cycle):
    core, row, _ = spot(cycle)
    n = image.shape[0]
    far = STEPS * n
    loads = [
        copy(t2_h, texts.at[0:n], sem.at[0]),
        copy(image_h.at[0:n], image, sem.at[1]),
        copy(image_h.at[n : n + TAIL], tail, sem.at[2]),
        copy(gi0_h, gi, sem.at[3]),
    ]
    start(*loads)

    @pl.when(core == 1)
    def _():
        copy(bx_h, texts.at[n : 2 * n], sem.at[4]).start()

    @pl.when(row == 0)
    def _():
        copy(edge_h, texts.at[2 * n : 3 * n], sem.at[5]).start()

    wait(*loads)
    rel = decode(tail[...], n)

    @pl.when(core == 0)
    def _():
        low, sums = pair(par, texts[0:n, :], image[...], rel, rows(n, far + 2 * n), True)
        gi[...] += dot_tn(low, texts[0:n, :])
        st[0:3, :] = st0[0:3, :] + sums

    @pl.when(core == 1)
    def _():
        copy(bx_h, texts.at[n : 2 * n], sem.at[4]).wait()
        low, sums = pair(par, texts[0 : 2 * n, :], image[...], rel, rows(n, far + 2 * n, far + n), True)
        gi[...] += dot_tn(low, texts[0 : 2 * n, :])
        st[0:3, :] = st0[0:3, :] + sums

    @pl.when(row == 0)
    def _():
        copy(edge_h, texts.at[2 * n : 3 * n], sem.at[5]).wait()
        low, sums = pair(par, texts[2 * n : 3 * n, :], image[...], rel, rows(n, 2 * n), True)
        gi[...] += dot_tn(low, texts[2 * n : 3 * n, :])
        st[0:3, :] += sums

    done = copy(gi, gi_h, sem.at[6])
    done.start()
    done.wait()


def k_tail(par, st0, image_h, t2x_h, edgex_h, home_h, gi0_h, gi, st, texts, image, tail, home, g0, sem, *, cycle):
    core, row, _ = spot(cycle)
    n = image.shape[0]
    step = jnp.where(core == 0, n, 3 * n)
    loads = [
        copy(t2x_h, texts.at[0:n], sem.at[0]),
        copy(image_h.at[0:n], image, sem.at[1]),
        copy(image_h.at[n : n + TAIL], tail, sem.at[2]),
        copy(gi0_h, g0, sem.at[3]),
        copy(home_h, home, sem.at[4]),
    ]
    start(*loads)

    @pl.when(row == 0)
    def _():
        copy(edgex_h, texts.at[n : 2 * n], sem.at[5]).start()

    wait(*loads[0:3])
    rel = decode(tail[...], n)
    low, sums = pair(par, texts[0:n, :], image[...], rel, rows(n, STEPS * n + step), True)
    wait(*loads[3:])
    st[...] = st0[0:3, :] + sums

    @pl.when(row == 0)
    def _():
        copy(edgex_h, texts.at[n : 2 * n], sem.at[5]).wait()
        low, sums = pair(par, texts[n : 2 * n, :], image[...], rel, rows(n, step), True)
        g0[...] += dot_tn(low, texts[n : 2 * n, :])
        st[...] += sums

    mine = g0[...] + dot_tn(low, texts[0:n, :])

    @pl.when(core == 0)
    def _():
        gi[...] = par[0] * (mine + home[0:n, :].astype(jnp.float32))
        parts = home[n : n + TAIL, 0:n].astype(jnp.float32)
        st[...] += parts[0:3] + parts[3:6] + parts[6:9]

    @pl.when(core == 1)
    def _():
        gi[...] = par[0] * mine


def on_device(image_emb, text_emb, labels, logit_params):
    n, d = image_emb.shape
    groups = lax.axis_size("grp")
    cycle = lax.axis_size("blk")
    half = cycle // 2
    last = half // 2 - 1
    tie = lax.optimization_barrier

    def row_of(k):
        return k % half // 2

    def inner(k):
        return 0 < row_of(k) < last

    def send(value, pairs):
        return lax.ppermute(value, AXES, pairs)

    def moves(dg, dk, keep=lambda k: True):
        return [
            (g * cycle + k, (g + dg) % groups * cycle + (k + dk) % cycle)
            for g in range(groups)
            for k in range(cycle)
            if keep(k)
        ]

    swap = moves(0, 1, lambda k: k % 2 == 0) + moves(0, -1, lambda k: k % 2 == 1)

    par = logit_params
    f32 = jax.ShapeDtypeStruct((n, d), jnp.float32)
    low = jax.ShapeDtypeStruct((n, d), jnp.bfloat16)
    full = jax.ShapeDtypeStruct((n + TAIL, d), jnp.bfloat16)
    stat = jax.ShapeDtypeStruct((8, n), jnp.float32)
    smem = pl.BlockSpec(memory_space=pltpu.SMEM)
    vmem = pl.BlockSpec(memory_space=pltpu.VMEM)
    hbm = pl.BlockSpec(memory_space=pltpu.HBM)

    def block(parts=1):
        return pltpu.VMEM((parts * n, d), jnp.bfloat16)

    def tails(parts=1):
        return pltpu.VMEM((parts * TAIL, d), jnp.bfloat16)

    total = pltpu.VMEM((n, d), jnp.float32)

    def call(body, params, small, big, outs, out_specs, scratch, sems, units, alias=None):
        return pl.pallas_call(
            functools.partial(body, cycle=cycle),
            out_shape=outs,
            in_specs=[smem] * len(params) + [vmem] * len(small) + [hbm] * len(big),
            out_specs=out_specs,
            scratch_shapes=[*scratch, pltpu.SemaphoreType.DMA((sems,))] if sems else [],
            input_output_aliases=alias or {},
            compiler_params=pltpu.CompilerParams(vmem_limit_bytes=56 * 1024 * 1024),
            cost_estimate=pl.CostEstimate(flops=units, bytes_accessed=units, transcendentals=0),
        )(*params, *small, *big)

    t1 = send(text_emb, moves(0, 2, lambda k: row_of(k) != last))
    b_in = send(text_emb, moves(1, 0, lambda k: row_of(k) != 0))
    image, other, leaves = call(
        functools.partial(k_pack, groups=groups), [], [labels.reshape(1, n)], [image_emb, text_emb], [full] * 3, [hbm] * 3,
        [block(), block(), tails()], 8, 0,
    )
    i1 = send(image, moves(0, -2))
    other = send(other, swap)
    g_img, g_txt, stats = call(
        k_first, [par], [], [image, text_emb, other], [f32, f32, stat], [hbm, hbm, vmem],
        [block(), tails(), block(), block(), tails(), total, total], 7, 5,
    )
    t1, i1, b_in, leaves, text, image, g_img = tie((t1, i1, b_in, leaves, text_emb, image, g_img))

    b_out = send(leaves, moves(1, 0, lambda k: row_of(k) == 0) + moves(0, -3, lambda k: k % half == 2))
    t2_over = send(t1, moves(1, 0, lambda k: row_of(k) == 1))
    mix = call(k_mix, [], [], [b_in, text], low, hbm, [block()], 2, 0)
    t2_mix = send(mix, moves(0, 2, inner) + moves(1, 2, lambda k: row_of(k) == last))
    t1x = send(t1, swap)
    i1x = send(i1, swap)
    t1x, i1x, i1s, text_s = tie((t1x, i1x, i1, text))
    i2 = send(i1s, moves(0, -1, lambda k: k % 2 == 0 and k % half != 0))
    edge = send(text_s, moves(0, 2, lambda k: row_of(k) == last))
    g_img, g_txt, stats = call(
        k_second, [par], [stats], [image, text, t1, t1x, i1, i1x, g_img, g_txt], [f32, f32, stat], [hbm, hbm, vmem],
        [block(), tails(), block(), block(2), block(2), tails(2), total, total], 13, 8, {8: 0, 9: 1},
    )

    b_out, b_in, g_img, g_txt = tie((b_out, b_in, g_img, g_txt))
    cross, b0 = call(
        k_cross, [par], [], [b_in, b_out, image, other, i1, i1x, i2], [low, low], [vmem, hbm],
        [block(), block(4), tails(4)], 10, 8,
    )
    back = send(cross, moves(-1, 0))
    bx = send(b0, moves(0, 1, lambda k: k % 2 == 0))
    g_img, g_txt, stats = call(
        k_mid, [par], [stats], [b0, image, text, i2, b_out, g_img, g_txt], [f32, f32, stat], [hbm, hbm, vmem],
        [block(), block(), tails(), block(), block(), tails(), total, total], 11, 0, {7: 0, 8: 1},
    )
    t2_mix, t2_over, edge, g_img = tie((t2_mix, t2_over, edge, g_img))
    away, t2 = call(
        k_away, [par], [], [i1x, t1, edge, t2_over, t2_mix], [full, low], [hbm, hbm],
        [block(), tails(), block(2), pltpu.VMEM((n + TAIL, d), jnp.bfloat16)], 6, 4,
    )
    home = send(away, moves(0, 1, lambda k: k % 2 == 1))
    t2x = send(t2, swap)
    edgex = send(edge, [p for p in swap if row_of(p[0] % cycle) == 0])
    g_img, stats = call(
        k_late, [par], [stats], [image, t2, bx, edge, g_img], [f32, stat], [hbm, vmem],
        [block(3), block(), tails(), total], 7, 0, {6: 0},
    )
    grad_text = logit_params[0] * (g_txt + back.astype(jnp.float32))
    grad_text, home, t2x, edgex = tie((grad_text, home, t2x, edgex))
    grad_image, stats = call(
        k_tail, [par], [stats], [image, t2x, edgex, home, g_img], [f32, jax.ShapeDtypeStruct((3, n), jnp.float32)],
        [vmem, vmem], [block(2), block(), tails(), pltpu.VMEM((n + TAIL, d), jnp.bfloat16), total], 6, 0,
    )
    return grad_image, grad_text, stats


def solution(mesh):
    return jax.shard_map(
        on_device,
        mesh=mesh,
        in_specs=(P(AXES, None), P(AXES, None), P(AXES), P()),
        out_specs=(P(AXES, None), P(AXES, None), P(None, AXES)),
        check_vma=False,
    )
```

```python
import functools

import jax
import jax.numpy as jnp
from jax import lax
from jax.experimental import pallas as pl
from jax.experimental.pallas import tpu as pltpu
from jax.sharding import PartitionSpec as P

STEPS = 4
AXES = ("grp", "blk")
TAIL = 16


def dot_nt(a, b):
    return lax.dot_general(a, b, (((1,), (1,)), ((), ())), preferred_element_type=jnp.float32)


def dot_nn(a, b):
    return lax.dot_general(a, b, (((1,), (0,)), ((), ())), preferred_element_type=jnp.float32)


def dot_tn(a, b):
    return lax.dot_general(a, b, (((0,), (0,)), ((), ())), preferred_element_type=jnp.float32)


def spot(cycle):
    place = lax.axis_index("blk")
    return lax.rem(place, 2), lax.div(lax.rem(place, cycle // 2), 2), cycle // 4 - 1


def decode(tail, n):
    codes = tail[:, 0:n].astype(jnp.float32)
    return codes[0:1, :] * 64.0 + codes[1:2, :]


def pair(par, texts, images, rel, row, want_stats):
    scale, bias = par[0], par[1]
    raw = dot_nt(texts, images)
    z = scale * raw + bias
    pos = rel == row
    e = jnp.exp(-jnp.abs(z))
    part = 1.0 / (1.0 + e)
    sig = jnp.where(z >= 0.0, part, e * part)
    grad = jnp.where(pos, sig - 1.0, sig)
    low = grad.astype(jnp.bfloat16)
    if not want_stats:
        return low, None
    loss = jnp.maximum(jnp.where(pos, -z, z), 0.0) + jnp.log1p(e)
    sums = [jnp.sum(v, axis=0, keepdims=True) for v in (loss, grad, grad * raw)]
    return low, jnp.concatenate(sums, axis=0)


def rows(n, *bases):
    one = lax.broadcasted_iota(jnp.int32, (n, 1), 0)
    return jnp.concatenate([one + b for b in bases], axis=0).astype(jnp.float32)


def copy(source, target, sem):
    return pltpu.make_async_copy(source, target, sem)


def start(*copies):
    for c in copies:
        c.start()


def wait(*copies):
    for c in copies:
        c.wait()


def k_pack(label, image_h, text_h, full_h, other_h, out_h, image, text, code, sem, *, cycle, groups):
    core, row, _ = spot(cycle)
    n = image.shape[0]
    load_i, load_t = copy(image_h, image, sem.at[0]), copy(text_h, text, sem.at[1])
    start(load_i, load_t)
    here = label[...].reshape(1, n)
    owner = lax.div(here, n)
    rnd = lax.rem(lax.axis_index("grp") - lax.div(owner, cycle) + groups, groups)
    step = lax.rem(lax.axis_index("blk") - lax.rem(owner, cycle) + cycle, cycle)
    rel = rnd * (STEPS * n) + step * n + lax.rem(here, n)
    code[...] = jnp.zeros(code.shape, jnp.bfloat16)
    fill = jnp.zeros((TAIL - 2, n), jnp.float32)
    parts = [lax.div(rel, 64).astype(jnp.float32), lax.rem(rel, 64).astype(jnp.float32), fill]
    code[:, 0:n] = jnp.concatenate(parts, axis=0).astype(jnp.bfloat16)
    marks = [copy(code, t.at[n : n + TAIL], sem.at[q + 2]) for q, t in enumerate((full_h, other_h, out_h))]
    start(*marks)
    wait(load_i, load_t)
    whole = copy(image, full_h.at[0:n], sem.at[5])
    whole.start()

    @pl.when(core == 0)
    def _():
        copy(text, other_h.at[0:n], sem.at[6]).start()

    @pl.when(core == 1)
    def _():
        copy(image, other_h.at[0:n], sem.at[6]).start()

    @pl.when((core == 0) & (row == 1))
    def _():
        copy(image, out_h.at[0:n], sem.at[7]).start()

    @pl.when((core == 1) | (row != 1))
    def _():
        copy(text, out_h.at[0:n], sem.at[7]).start()

    wait(*marks, whole)
    copy(text, other_h.at[0:n], sem.at[6]).wait()
    copy(text, out_h.at[0:n], sem.at[7]).wait()


def k_mix(inner_h, text_h, out_h, hold, sem, *, cycle):
    _, row, last = spot(cycle)

    @pl.when(row != last)
    def _():
        copy(inner_h, hold, sem.at[0]).start()

    @pl.when(row == last)
    def _():
        copy(text_h, hold, sem.at[0]).start()

    copy(inner_h, hold, sem.at[0]).wait()
    out = copy(hold, out_h, sem.at[1])
    out.start()
    out.wait()


def k_first(par, image_h, text_h, other_h, gi_h, gt_h, st, image, tail, text, extra, etail, gi, gt, sem, *, cycle):
    core, _, _ = spot(cycle)
    n = text.shape[0]
    loads = [
        copy(image_h.at[0:n], image, sem.at[0]),
        copy(image_h.at[n : n + TAIL], tail, sem.at[1]),
        copy(text_h, text, sem.at[2]),
        copy(other_h.at[0:n], extra, sem.at[3]),
        copy(other_h.at[n : n + TAIL], etail, sem.at[4]),
    ]
    start(*loads)
    wait(*loads[0:3])
    rel = decode(tail[...], n)
    low, sums = pair(par, text[...], image[...], rel, rows(n, 0), True)
    gt[...] = dot_nn(low, image[...])
    gi[...] = dot_tn(low, text[...])
    st[0:3, :] = sums
    wait(*loads[3:])

    @pl.when(core == 1)
    def _():
        low, sums = pair(par, extra[...], image[...], rel, rows(n, n), True)
        gi[...] += dot_tn(low, extra[...])
        st[0:3, :] += sums

    @pl.when(core == 0)
    def _():
        low, _ = pair(par, text[...], extra[...], decode(etail[...], n), rows(n, n), False)
        gt[...] += dot_nn(low, extra[...])

    out = [copy(gi, gi_h, sem.at[5]), copy(gt, gt_h, sem.at[6])]
    start(*out)
    wait(*out)


def k_second(
    par, st0, image_h, text_h, t1_h, t1x_h, i1_h, i1x_h, gi0_h, gt0_h, gi_h, gt_h, st,
    image, tail, text, texts, images, tails, gi, gt, sem, *, cycle,
):
    core, row, _ = spot(cycle)
    n = text.shape[0]
    near = core == 0
    loads = [
        copy(image_h.at[0:n], image, sem.at[0]),
        copy(image_h.at[n : n + TAIL], tail, sem.at[1]),
        copy(t1_h, texts.at[0:n], sem.at[2]),
        copy(t1x_h, texts.at[n : 2 * n], sem.at[3]),
        copy(gi0_h, gi, sem.at[4]),
    ]
    more = [
        copy(text_h, text, sem.at[5]),
        copy(i1_h.at[0:n], images.at[0:n], sem.at[6]),
        copy(i1_h.at[n : n + TAIL], tails.at[0:TAIL], sem.at[7]),
        copy(i1x_h.at[0:n], images.at[n : 2 * n], sem.at[8]),
        copy(i1x_h.at[n : n + TAIL], tails.at[TAIL : 2 * TAIL], sem.at[9]),
        copy(gt0_h, gt, sem.at[10]),
    ]
    out_i = copy(gi, gi_h, sem.at[11])
    start(*loads, *more)
    wait(*loads)

    @pl.when(row > 0)
    def _():
        row_i = rows(n, 2 * n, jnp.where(near, n, 3 * n))
        low, sums = pair(par, texts[...], image[...], decode(tail[...], n), row_i, True)
        gi[...] += dot_tn(low, texts[...])
        st[0:3, :] = st0[0:3, :] + sums

    @pl.when(row == 0)
    def _():
        st[0:3, :] = st0[0:3, :]

    out_i.start()
    wait(*more)
    rel = jnp.concatenate(
        [
            decode(tails[0:TAIL, :], n) - jnp.float32(2 * n),
            decode(tails[TAIL : 2 * TAIL, :], n) - jnp.where(near, 3 * n, n).astype(jnp.float32),
        ],
        axis=1,
    )
    low, _ = pair(par, text[...], images[...], rel, rows(n, 0), False)
    gt[...] += dot_nn(low, images[...])
    out_t = copy(gt, gt_h, sem.at[12])
    out_t.start()
    wait(out_i, out_t)


def k_cross(
    par, inner_h, out_h, image_h, other_h, i1_h, i1x_h, i2_h, out, b0_h,
    text, images, tails, sem, *, cycle,
):
    core, row, last = spot(cycle)
    n = text.shape[0]
    near = core == 0

    def part(source, q):
        return (
            copy(source.at[0:n], images.at[q * n : (q + 1) * n], sem.at[2 * q]),
            copy(source.at[n : n + TAIL], tails.at[q * TAIL : (q + 1) * TAIL], sem.at[2 * q + 1]),
        )

    @pl.when(row == 0)
    def _():
        copy(out_h.at[0:n], text, sem.at[8]).start()

    @pl.when(row > 0)
    def _():
        copy(inner_h, text, sem.at[8]).start()

    for q, source in enumerate((image_h, i1_h, i1x_h)):
        start(*part(source, q))

    @pl.when(near)
    def _():
        start(*part(other_h, 3))

    @pl.when((core == 1) & (row != last))
    def _():
        start(*part(i2_h, 3))

    @pl.when((core == 1) & (row == last))
    def _():
        start(*part(out_h, 3))

    copy(inner_h, text, sem.at[8]).wait()
    keep = copy(text, b0_h, sem.at[9])
    keep.start()
    for q in range(4):
        wait(*part(image_h, q))
    steps = (0, 2 * n, jnp.where(near, 3 * n, n), jnp.where(near, n, 3 * n))
    rel = [
        decode(tails[q * TAIL : (q + 1) * TAIL, :], n) - jnp.asarray(s + STEPS * n, jnp.float32)
        for q, s in enumerate(steps)
    ]
    row_t = rows(n, 0)
    first, _ = pair(par, text[...], images[0 : 2 * n, :], jnp.concatenate(rel[0:2], axis=1), row_t, False)
    second, _ = pair(par, text[...], images[2 * n : 4 * n, :], jnp.concatenate(rel[2:4], axis=1), row_t, False)
    out[...] = dot_nn(jnp.concatenate([first, second], axis=1), images[...]).astype(jnp.bfloat16)
    keep.wait()


def k_away(par, image_h, t1_h, edge_h, over_h, mix_h, out_h, t2_h, image, tail, texts, out, sem, *, cycle):
    core, row, _ = spot(cycle)
    n = t1_h.shape[0]
    first, second = texts.at[0:n], texts.at[n : 2 * n]

    @pl.when(row == 1)
    def _():
        copy(over_h, second, sem.at[0]).start()

    @pl.when(row != 1)
    def _():
        copy(mix_h, second, sem.at[0]).start()

    @pl.when(row == 0)
    def _():
        copy(edge_h, first, sem.at[3]).start()

    @pl.when(row != 0)
    def _():
        copy(t1_h, first, sem.at[3]).start()

    loads = [copy(image_h.at[0:n], image, sem.at[1]), copy(image_h.at[n : n + TAIL], tail, sem.at[2])]
    start(*loads)
    copy(mix_h, second, sem.at[0]).wait()
    keep = copy(second, t2_h, sem.at[4])
    keep.start()
    copy(t1_h, first, sem.at[3]).wait()
    wait(*loads)

    @pl.when(core == 1)
    def _():
        row_i = rows(n, 3 * n, (STEPS + 3) * n)
        low, sums = pair(par, texts[...], image[...], decode(tail[...], n), row_i, True)
        out[0:n, :] = dot_tn(low, texts[...]).astype(jnp.bfloat16)
        high = sums.astype(jnp.bfloat16)
        rest = sums - high.astype(jnp.float32)
        mid = rest.astype(jnp.bfloat16)
        end = (rest - mid.astype(jnp.float32)).astype(jnp.bfloat16)
        fill = jnp.zeros((TAIL - 9, n), jnp.bfloat16)
        out[n : n + TAIL, :] = jnp.zeros((TAIL, out.shape[1]), jnp.bfloat16)
        out[n : n + TAIL, 0:n] = jnp.concatenate([high, mid, end, fill], axis=0)
        done = copy(out, out_h, sem.at[5])
        done.start()
        done.wait()

    keep.wait()


def k_mid(
    par, st0, b0_h, image_h, text_h, i2_h, out_h, gi0_h, gt0_h, gi_h, gt_h, st,
    b0, image, tail, text, extra, etail, gi, gt, sem, *, cycle,
):
    core, row, last = spot(cycle)
    n = text.shape[0]
    loads = [
        copy(b0_h, b0, sem.at[0]),
        copy(image_h.at[0:n], image, sem.at[1]),
        copy(image_h.at[n : n + TAIL], tail, sem.at[2]),
        copy(gi0_h, gi, sem.at[3]),
    ]
    start(*loads)

    @pl.when(core == 1)
    def _():
        start(copy(text_h, text, sem.at[5]), copy(gt0_h, gt, sem.at[6]))

    @pl.when((core == 1) & (row != last))
    def _():
        start(copy(i2_h.at[0:n], extra, sem.at[7]), copy(i2_h.at[n : n + TAIL], etail, sem.at[8]))

    @pl.when((core == 1) & (row == last))
    def _():
        start(copy(out_h.at[0:n], extra, sem.at[7]), copy(out_h.at[n : n + TAIL], etail, sem.at[8]))

    wait(*loads)
    low, sums = pair(par, b0[...], image[...], decode(tail[...], n), rows(n, STEPS * n), True)
    gi[...] += dot_tn(low, b0[...])
    st[0:3, :] = st0[0:3, :] + sums
    done = copy(gi, gi_h, sem.at[10])
    done.start()

    @pl.when(core == 1)
    def _():
        wait(copy(text_h, text, sem.at[5]), copy(gt0_h, gt, sem.at[6]))
        wait(copy(i2_h.at[0:n], extra, sem.at[7]), copy(i2_h.at[n : n + TAIL], etail, sem.at[8]))
        low, _ = pair(par, text[...], extra[...], decode(etail[...], n), rows(n, 3 * n), False)
        gt[...] += dot_nn(low, extra[...])
        copy(gt, gt_h, sem.at[9]).start()
        copy(gt, gt_h, sem.at[9]).wait()

    done.wait()


def k_late(par, st0, image_h, t2_h, bx_h, edge_h, gi0_h, gi_h, st, texts, image, tail, gi, sem, *, cycle):
    core, row, _ = spot(cycle)
    n = image.shape[0]
    far = STEPS * n
    loads = [
        copy(t2_h, texts.at[0:n], sem.at[0]),
        copy(image_h.at[0:n], image, sem.at[1]),
        copy(image_h.at[n : n + TAIL], tail, sem.at[2]),
        copy(gi0_h, gi, sem.at[3]),
    ]
    start(*loads)

    @pl.when(core == 1)
    def _():
        copy(bx_h, texts.at[n : 2 * n], sem.at[4]).start()

    @pl.when(row == 0)
    def _():
        copy(edge_h, texts.at[2 * n : 3 * n], sem.at[5]).start()

    wait(*loads)
    rel = decode(tail[...], n)

    @pl.when(core == 0)
    def _():
        low, sums = pair(par, texts[0:n, :], image[...], rel, rows(n, far + 2 * n), True)
        gi[...] += dot_tn(low, texts[0:n, :])
        st[0:3, :] = st0[0:3, :] + sums

    @pl.when(core == 1)
    def _():
        copy(bx_h, texts.at[n : 2 * n], sem.at[4]).wait()
        low, sums = pair(par, texts[0 : 2 * n, :], image[...], rel, rows(n, far + 2 * n, far + n), True)
        gi[...] += dot_tn(low, texts[0 : 2 * n, :])
        st[0:3, :] = st0[0:3, :] + sums

    @pl.when(row == 0)
    def _():
        copy(edge_h, texts.at[2 * n : 3 * n], sem.at[5]).wait()
        low, sums = pair(par, texts[2 * n : 3 * n, :], image[...], rel, rows(n, 2 * n), True)
        gi[...] += dot_tn(low, texts[2 * n : 3 * n, :])
        st[0:3, :] += sums

    done = copy(gi, gi_h, sem.at[6])
    done.start()
    done.wait()


def k_tail(par, st0, image_h, t2x_h, edgex_h, home_h, gi0_h, gi, st, texts, image, tail, home, g0, sem, *, cycle):
    core, row, _ = spot(cycle)
    n = image.shape[0]
    step = jnp.where(core == 0, n, 3 * n)
    loads = [
        copy(t2x_h, texts.at[0:n], sem.at[0]),
        copy(image_h.at[0:n], image, sem.at[1]),
        copy(image_h.at[n : n + TAIL], tail, sem.at[2]),
        copy(gi0_h, g0, sem.at[3]),
        copy(home_h, home, sem.at[4]),
    ]
    start(*loads)

    @pl.when(row == 0)
    def _():
        copy(edgex_h, texts.at[n : 2 * n], sem.at[5]).start()

    wait(*loads[0:3])
    rel = decode(tail[...], n)
    low, sums = pair(par, texts[0:n, :], image[...], rel, rows(n, STEPS * n + step), True)
    wait(*loads[3:])
    st[...] = st0[0:3, :] + sums

    @pl.when(row == 0)
    def _():
        copy(edgex_h, texts.at[n : 2 * n], sem.at[5]).wait()
        low, sums = pair(par, texts[n : 2 * n, :], image[...], rel, rows(n, step), True)
        g0[...] += dot_tn(low, texts[n : 2 * n, :])
        st[...] += sums

    mine = g0[...] + dot_tn(low, texts[0:n, :])

    @pl.when(core == 0)
    def _():
        gi[...] = par[0] * (mine + home[0:n, :].astype(jnp.float32))
        parts = home[n : n + TAIL, 0:n].astype(jnp.float32)
        st[...] += parts[0:3] + parts[3:6] + parts[6:9]

    @pl.when(core == 1)
    def _():
        gi[...] = par[0] * mine


def on_device(image_emb, text_emb, labels, logit_params):
    n, d = image_emb.shape
    groups = lax.axis_size("grp")
    cycle = lax.axis_size("blk")
    half = cycle // 2
    last = half // 2 - 1
    tie = lax.optimization_barrier

    def row_of(k):
        return k % half // 2

    def inner(k):
        return 0 < row_of(k) < last

    def send(value, pairs):
        return lax.ppermute(value, AXES, pairs)

    def moves(dg, dk, keep=lambda k: True):
        return [
            (g * cycle + k, (g + dg) % groups * cycle + (k + dk) % cycle)
            for g in range(groups)
            for k in range(cycle)
            if keep(k)
        ]

    swap = moves(0, 1, lambda k: k % 2 == 0) + moves(0, -1, lambda k: k % 2 == 1)

    par = logit_params
    f32 = jax.ShapeDtypeStruct((n, d), jnp.float32)
    low = jax.ShapeDtypeStruct((n, d), jnp.bfloat16)
    full = jax.ShapeDtypeStruct((n + TAIL, d), jnp.bfloat16)
    stat = jax.ShapeDtypeStruct((8, n), jnp.float32)
    smem = pl.BlockSpec(memory_space=pltpu.SMEM)
    vmem = pl.BlockSpec(memory_space=pltpu.VMEM)
    hbm = pl.BlockSpec(memory_space=pl.ANY)

    def block(parts=1):
        return pltpu.VMEM((parts * n, d), jnp.bfloat16)

    def tails(parts=1):
        return pltpu.VMEM((parts * TAIL, d), jnp.bfloat16)

    total = pltpu.VMEM((n, d), jnp.float32)

    def call(body, params, small, big, outs, out_specs, scratch, sems, units, alias=None):
        return pl.pallas_call(
            functools.partial(body, cycle=cycle),
            out_shape=outs,
            in_specs=[smem] * len(params) + [vmem] * len(small) + [hbm] * len(big),
            out_specs=out_specs,
            scratch_shapes=[*scratch, pltpu.SemaphoreType.DMA((sems,))] if sems else [],
            input_output_aliases=alias or {},
            compiler_params=pltpu.CompilerParams(vmem_limit_bytes=24 * 1024 * 1024),
            cost_estimate=pl.CostEstimate(flops=units, bytes_accessed=units, transcendentals=0),
        )(*params, *small, *big)

    t1 = send(text_emb, moves(0, 2, lambda k: row_of(k) != last))
    b_in = send(text_emb, moves(1, 0, lambda k: row_of(k) != 0))
    image, other, leaves = call(
        functools.partial(k_pack, groups=groups), [], [labels], [image_emb, text_emb], [full] * 3, [hbm] * 3,
        [block(), block(), tails()], 8, 0,
    )
    i1 = send(image, moves(0, -2))
    other = send(other, swap)
    g_img, g_txt, stats = call(
        k_first, [par], [], [image, text_emb, other], [f32, f32, stat], [hbm, hbm, vmem],
        [block(), tails(), block(), block(), tails(), total, total], 7, 5,
    )
    t1, i1, b_in, leaves, text, image, g_img = tie((t1, i1, b_in, leaves, text_emb, image, g_img))

    b_out = send(leaves, moves(1, 0, lambda k: row_of(k) == 0) + moves(0, -3, lambda k: k % half == 2))
    mix = call(k_mix, [], [], [b_in, text], low, hbm, [block()], 2, 0)
    t2_mix = send(mix, moves(0, 2, inner) + moves(1, 2, lambda k: row_of(k) == last))
    t1x = send(t1, swap)
    i1x = send(i1, swap)
    t1x, i1x, i1s, text_s = tie((t1x, i1x, i1, text))
    i2 = send(i1s, moves(0, -1, lambda k: k % 2 == 0 and k % half != 0))
    edge = send(text_s, moves(0, 2, lambda k: row_of(k) == last))
    g_img, g_txt, stats = call(
        k_second, [par], [stats], [image, text, t1, t1x, i1, i1x, g_img, g_txt], [f32, f32, stat], [hbm, hbm, vmem],
        [block(), tails(), block(), block(2), block(2), tails(2), total, total], 13, 8, {8: 0, 9: 1},
    )

    t1_o, i2 = tie((t1, i2))
    t2_over = send(t1_o, moves(1, 0, lambda k: row_of(k) == 1))

    b_out, b_in, g_img, g_txt = tie((b_out, b_in, g_img, g_txt))
    cross, b0 = call(
        k_cross, [par], [], [b_in, b_out, image, other, i1, i1x, i2], [low, low], [vmem, hbm],
        [block(), block(4), tails(4)], 10, 8,
    )
    back = send(cross, moves(-1, 0))
    g_img, g_txt, stats = call(
        k_mid, [par], [stats], [b0, image, text, i2, b_out, g_img, g_txt], [f32, f32, stat], [hbm, hbm, vmem],
        [block(), block(), tails(), block(), block(), tails(), total, total], 11, 0, {7: 0, 8: 1},
    )
    t2_mix, t2_over, edge, g_img, b0 = tie((t2_mix, t2_over, edge, g_img, b0))
    bx = send(b0, moves(0, 1, lambda k: k % 2 == 0))
    away, t2 = call(
        k_away, [par], [], [i1x, t1, edge, t2_over, t2_mix], [full, low], [hbm, hbm],
        [block(), tails(), block(2), pltpu.VMEM((n + TAIL, d), jnp.bfloat16)], 6, 4,
    )
    home = send(away, moves(0, 1, lambda k: k % 2 == 1))
    t2x = send(t2, swap)
    edgex = send(edge, [p for p in swap if row_of(p[0] % cycle) == 0])
    g_img, stats = call(
        k_late, [par], [stats], [image, t2, bx, edge, g_img], [f32, stat], [hbm, vmem],
        [block(3), block(), tails(), total], 7, 0, {6: 0},
    )
    grad_text = logit_params[0] * (g_txt + back.astype(jnp.float32))
    grad_text, home, t2x, edgex = tie((grad_text, home, t2x, edgex))
    grad_image, stats = call(
        k_tail, [par], [stats], [image, t2x, edgex, home, g_img], [f32, jax.ShapeDtypeStruct((3, n), jnp.float32)],
        [vmem, vmem], [block(2), block(), tails(), pltpu.VMEM((n + TAIL, d), jnp.bfloat16), total], 6, 0,
    )
    return grad_image, grad_text, stats


def solution(mesh):
    return jax.shard_map(
        on_device,
        mesh=mesh,
        in_specs=(P(AXES, None), P(AXES, None), P(AXES), P()),
        out_specs=(P(AXES, None), P(AXES, None), P(None, AXES)),
        check_vma=False,
    )
```

```python
import functools

import jax
import jax.numpy as jnp
from jax import lax
from jax.experimental import pallas as pl
from jax.experimental.pallas import tpu as pltpu
from jax.sharding import PartitionSpec as P

STEPS = 4
AXES = ("grp", "blk")
TAIL = 16


def dot_nt(a, b):
    return lax.dot_general(a, b, (((1,), (1,)), ((), ())), preferred_element_type=jnp.float32)


def dot_nn(a, b):
    return lax.dot_general(a, b, (((1,), (0,)), ((), ())), preferred_element_type=jnp.float32)


def dot_tn(a, b):
    return lax.dot_general(a, b, (((0,), (0,)), ((), ())), preferred_element_type=jnp.float32)


def spot(cycle):
    place = lax.axis_index("blk")
    return lax.rem(place, 2), lax.div(lax.rem(place, cycle // 2), 2), cycle // 4 - 1


def decode(tail, n):
    codes = tail[:, 0:n].astype(jnp.float32)
    return codes[0:1, :] * 64.0 + codes[1:2, :]


def pair(par, texts, images, rel, row, want_stats):
    scale, bias = par[0], par[1]
    raw = dot_nt(texts, images)
    z = scale * raw + bias
    pos = rel == row
    e = jnp.exp(-jnp.abs(z))
    part = 1.0 / (1.0 + e)
    sig = jnp.where(z >= 0.0, part, e * part)
    grad = jnp.where(pos, sig - 1.0, sig)
    low = grad.astype(jnp.bfloat16)
    if not want_stats:
        return low, None
    loss = jnp.maximum(jnp.where(pos, -z, z), 0.0) + jnp.log1p(e)
    sums = [jnp.sum(v, axis=0, keepdims=True) for v in (loss, grad, grad * raw)]
    return low, jnp.concatenate(sums, axis=0)


def rows(n, *bases):
    one = lax.broadcasted_iota(jnp.int32, (n, 1), 0)
    return jnp.concatenate([one + b for b in bases], axis=0).astype(jnp.float32)


def copy(source, target, sem):
    return pltpu.make_async_copy(source, target, sem)


def start(*copies):
    for c in copies:
        c.start()


def wait(*copies):
    for c in copies:
        c.wait()


def k_pack(label, image_h, text_h, full_h, other_h, out_h, image, text, code, sem, *, cycle, groups):
    core, row, _ = spot(cycle)
    n = image.shape[0]
    load_i, load_t = copy(image_h, image, sem.at[0]), copy(text_h, text, sem.at[1])
    start(load_i, load_t)
    here = label[...].reshape(1, n)
    owner = lax.div(here, n)
    rnd = lax.rem(lax.axis_index("grp") - lax.div(owner, cycle) + groups, groups)
    step = lax.rem(lax.axis_index("blk") - lax.rem(owner, cycle) + cycle, cycle)
    rel = rnd * (STEPS * n) + step * n + lax.rem(here, n)
    code[...] = jnp.zeros(code.shape, jnp.bfloat16)
    fill = jnp.zeros((TAIL - 2, n), jnp.float32)
    parts = [lax.div(rel, 64).astype(jnp.float32), lax.rem(rel, 64).astype(jnp.float32), fill]
    code[:, 0:n] = jnp.concatenate(parts, axis=0).astype(jnp.bfloat16)
    marks = [copy(code, t.at[n : n + TAIL], sem.at[q + 2]) for q, t in enumerate((full_h, other_h, out_h))]
    start(*marks)
    wait(load_i, load_t)
    whole = copy(image, full_h.at[0:n], sem.at[5])
    whole.start()

    @pl.when(core == 0)
    def _():
        copy(text, other_h.at[0:n], sem.at[6]).start()

    @pl.when(core == 1)
    def _():
        copy(image, other_h.at[0:n], sem.at[6]).start()

    @pl.when((core == 0) & (row == 1))
    def _():
        copy(image, out_h.at[0:n], sem.at[7]).start()

    @pl.when((core == 1) | (row != 1))
    def _():
        copy(text, out_h.at[0:n], sem.at[7]).start()

    wait(*marks, whole)
    copy(text, other_h.at[0:n], sem.at[6]).wait()
    copy(text, out_h.at[0:n], sem.at[7]).wait()


def k_mix(inner_h, text_h, out_h, hold, sem, *, cycle):
    _, row, last = spot(cycle)

    @pl.when(row != last)
    def _():
        copy(inner_h, hold, sem.at[0]).start()

    @pl.when(row == last)
    def _():
        copy(text_h, hold, sem.at[0]).start()

    copy(inner_h, hold, sem.at[0]).wait()
    out = copy(hold, out_h, sem.at[1])
    out.start()
    out.wait()


def k_first(par, image_h, text_h, other_h, gi_h, gt_h, st, image, tail, text, extra, etail, gi, gt, sem, *, cycle):
    core, _, _ = spot(cycle)
    n = text.shape[0]
    loads = [
        copy(image_h.at[0:n], image, sem.at[0]),
        copy(image_h.at[n : n + TAIL], tail, sem.at[1]),
        copy(text_h, text, sem.at[2]),
        copy(other_h.at[0:n], extra, sem.at[3]),
        copy(other_h.at[n : n + TAIL], etail, sem.at[4]),
    ]
    start(*loads)
    wait(*loads[0:3])
    rel = decode(tail[...], n)
    low, sums = pair(par, text[...], image[...], rel, rows(n, 0), True)
    gt[...] = dot_nn(low, image[...])
    gi[...] = dot_tn(low, text[...])
    st[0:3, :] = sums
    wait(*loads[3:])

    @pl.when(core == 1)
    def _():
        low, sums = pair(par, extra[...], image[...], rel, rows(n, n), True)
        gi[...] += dot_tn(low, extra[...])
        st[0:3, :] += sums

    @pl.when(core == 0)
    def _():
        low, _ = pair(par, text[...], extra[...], decode(etail[...], n), rows(n, n), False)
        gt[...] += dot_nn(low, extra[...])

    out = [copy(gi, gi_h, sem.at[5]), copy(gt, gt_h, sem.at[6])]
    start(*out)
    wait(*out)


def k_second(
    par, st0, image_h, text_h, t1_h, t1x_h, i1_h, i1x_h, gi0_h, gt0_h, gi_h, gt_h, st,
    image, tail, text, texts, images, tails, gi, gt, sem, *, cycle,
):
    core, row, _ = spot(cycle)
    n = text.shape[0]
    near = core == 0
    loads = [
        copy(image_h.at[0:n], image, sem.at[0]),
        copy(image_h.at[n : n + TAIL], tail, sem.at[1]),
        copy(gi0_h, gi, sem.at[4]),
    ]

    @pl.when((row > 0) | near)
    def _():
        copy(t1_h, texts.at[0:n], sem.at[2]).start()

    @pl.when((row == 0) & (core == 1))
    def _():
        copy(t1x_h, texts.at[0:n], sem.at[2]).start()

    @pl.when(row > 0)
    def _():
        copy(t1x_h, texts.at[n : 2 * n], sem.at[3]).start()

    more = [
        copy(text_h, text, sem.at[5]),
        copy(i1_h.at[0:n], images.at[0:n], sem.at[6]),
        copy(i1_h.at[n : n + TAIL], tails.at[0:TAIL], sem.at[7]),
        copy(i1x_h.at[0:n], images.at[n : 2 * n], sem.at[8]),
        copy(i1x_h.at[n : n + TAIL], tails.at[TAIL : 2 * TAIL], sem.at[9]),
        copy(gt0_h, gt, sem.at[10]),
    ]
    out_i = copy(gi, gi_h, sem.at[11])
    start(*loads, *more)
    wait(*loads)
    copy(t1_h, texts.at[0:n], sem.at[2]).wait()

    @pl.when(row > 0)
    def _():
        copy(t1x_h, texts.at[n : 2 * n], sem.at[3]).wait()
        row_i = rows(n, 2 * n, jnp.where(near, n, 3 * n))
        low, sums = pair(par, texts[...], image[...], decode(tail[...], n), row_i, True)
        gi[...] += dot_tn(low, texts[...])
        st[0:3, :] = st0[0:3, :] + sums

    @pl.when(row == 0)
    def _():
        row_i = rows(n, jnp.where(near, 2 * n, 3 * n))
        low, sums = pair(par, texts[0:n, :], image[...], decode(tail[...], n), row_i, True)
        gi[...] += dot_tn(low, texts[0:n, :])
        st[0:3, :] = st0[0:3, :] + sums

    out_i.start()
    wait(*more)
    rel = jnp.concatenate(
        [
            decode(tails[0:TAIL, :], n) - jnp.float32(2 * n),
            decode(tails[TAIL : 2 * TAIL, :], n) - jnp.where(near, 3 * n, n).astype(jnp.float32),
        ],
        axis=1,
    )
    low, _ = pair(par, text[...], images[...], rel, rows(n, 0), False)
    gt[...] += dot_nn(low, images[...])
    out_t = copy(gt, gt_h, sem.at[12])
    out_t.start()
    wait(out_i, out_t)


def k_cross(
    par, inner_h, out_h, image_h, other_h, i1_h, i1x_h, i2_h, iw_h, out, b0_h,
    text, images, tails, sem, *, cycle,
):
    core, row, last = spot(cycle)
    n = text.shape[0]
    near = core == 0

    def part(source, q):
        return (
            copy(source.at[0:n], images.at[q * n : (q + 1) * n], sem.at[2 * q]),
            copy(source.at[n : n + TAIL], tails.at[q * TAIL : (q + 1) * TAIL], sem.at[2 * q + 1]),
        )

    late = (row == 0) | (row == last)

    @pl.when(late)
    def _():
        copy(out_h, text, sem.at[8]).start()

    @pl.when(jnp.logical_not(late))
    def _():
        copy(inner_h, text, sem.at[8]).start()

    for q, source in enumerate((image_h, i1_h, i1x_h)):
        start(*part(source, q))

    @pl.when(near)
    def _():
        start(*part(other_h, 3))

    @pl.when((core == 1) & (row != last))
    def _():
        start(*part(i2_h, 3))

    @pl.when((core == 1) & (row == last))
    def _():
        start(*part(iw_h, 3))

    copy(inner_h, text, sem.at[8]).wait()
    keep = copy(text, b0_h, sem.at[9])
    keep.start()
    for q in range(4):
        wait(*part(image_h, q))
    steps = (0, 2 * n, jnp.where(near, 3 * n, n), jnp.where(near, n, 3 * n))
    rel = [
        decode(tails[q * TAIL : (q + 1) * TAIL, :], n) - jnp.asarray(s + STEPS * n, jnp.float32)
        for q, s in enumerate(steps)
    ]
    row_t = rows(n, 0)
    first, _ = pair(par, text[...], images[0 : 2 * n, :], jnp.concatenate(rel[0:2], axis=1), row_t, False)
    second, _ = pair(par, text[...], images[2 * n : 4 * n, :], jnp.concatenate(rel[2:4], axis=1), row_t, False)
    out[...] = dot_nn(jnp.concatenate([first, second], axis=1), images[...]).astype(jnp.bfloat16)
    keep.wait()


def k_away(par, image_h, t1_h, edge_h, early_h, over_h, mix_h, out_h, t2_h, image, tail, texts, out, sem, *, cycle):
    core, row, _ = spot(cycle)
    n = t1_h.shape[0]
    first, second = texts.at[0:n], texts.at[n : 2 * n]

    @pl.when(row == 1)
    def _():
        copy(over_h, second, sem.at[0]).start()

    @pl.when((row == 0) & (core == 0))
    def _():
        copy(early_h, second, sem.at[0]).start()

    @pl.when((row > 1) | ((row == 0) & (core == 1)))
    def _():
        copy(mix_h, second, sem.at[0]).start()

    @pl.when(row == 0)
    def _():
        copy(edge_h.at[0:n], first, sem.at[3]).start()

    @pl.when(row != 0)
    def _():
        copy(t1_h, first, sem.at[3]).start()

    loads = [copy(image_h.at[0:n], image, sem.at[1]), copy(image_h.at[n : n + TAIL], tail, sem.at[2])]
    start(*loads)
    copy(mix_h, second, sem.at[0]).wait()
    keep = copy(second, t2_h, sem.at[4])
    keep.start()
    copy(t1_h, first, sem.at[3]).wait()
    wait(*loads)

    @pl.when(core == 1)
    def _():
        row_i = rows(n, 3 * n, (STEPS + 3) * n)
        low, sums = pair(par, texts[...], image[...], decode(tail[...], n), row_i, True)
        out[0:n, :] = dot_tn(low, texts[...]).astype(jnp.bfloat16)
        high = sums.astype(jnp.bfloat16)
        rest = sums - high.astype(jnp.float32)
        mid = rest.astype(jnp.bfloat16)
        end = (rest - mid.astype(jnp.float32)).astype(jnp.bfloat16)
        fill = jnp.zeros((TAIL - 9, n), jnp.bfloat16)
        out[n : n + TAIL, :] = jnp.zeros((TAIL, out.shape[1]), jnp.bfloat16)
        out[n : n + TAIL, 0:n] = jnp.concatenate([high, mid, end, fill], axis=0)
        done = copy(out, out_h, sem.at[5])
        done.start()
        done.wait()

    keep.wait()


def k_late(
    par, st0, b0_h, t2_h, edge_h, image_h, text_h, i2_h, gi0_h, gt0_h, gi_h, gt_h, st,
    texts, image, tail, text, extra, etail, gi, gt, sem, *, cycle,
):
    core, row, last = spot(cycle)
    n = text.shape[0]
    far = STEPS * n
    loads = [
        copy(b0_h, texts.at[0:n], sem.at[0]),
        copy(t2_h, texts.at[n : 2 * n], sem.at[1]),
        copy(image_h.at[0:n], image, sem.at[3]),
        copy(image_h.at[n : n + TAIL], tail, sem.at[4]),
        copy(gi0_h, gi, sem.at[5]),
    ]
    start(*loads)

    @pl.when(core == 1)
    def _():
        start(copy(text_h, text, sem.at[7]), copy(gt0_h, gt, sem.at[8]))

    @pl.when((core == 1) & (row != last))
    def _():
        start(copy(i2_h.at[0:n], extra, sem.at[9]), copy(i2_h.at[n : n + TAIL], etail, sem.at[10]))

    @pl.when((core == 1) & (row == last))
    def _():
        start(copy(edge_h.at[0:n], extra, sem.at[9]), copy(edge_h.at[n : n + TAIL], etail, sem.at[10]))

    @pl.when((row == 0) & (core == 1))
    def _():
        copy(edge_h.at[0:n], texts.at[2 * n : 3 * n], sem.at[11]).start()

    wait(*loads[0:4])
    rel = decode(tail[...], n)
    low, sums = pair(par, texts[0 : 2 * n, :], image[...], rel, rows(n, far, far + 2 * n), True)
    loads[4].wait()
    gi[...] += dot_tn(low, texts[0 : 2 * n, :])
    st[0:3, :] = st0[0:3, :] + sums

    @pl.when(core == 1)
    def _():
        wait(copy(text_h, text, sem.at[7]), copy(gt0_h, gt, sem.at[8]))
        wait(copy(i2_h.at[0:n], extra, sem.at[9]), copy(i2_h.at[n : n + TAIL], etail, sem.at[10]))
        low, _ = pair(par, text[...], extra[...], decode(etail[...], n), rows(n, 3 * n), False)
        gt[...] += dot_nn(low, extra[...])
        copy(gt, gt_h, sem.at[13]).start()

    @pl.when((row == 0) & (core == 1))
    def _():
        copy(edge_h.at[0:n], texts.at[2 * n : 3 * n], sem.at[11]).wait()
        low, sums = pair(par, texts[2 * n : 3 * n, :], image[...], rel, rows(n, 2 * n), True)
        gi[...] += dot_tn(low, texts[2 * n : 3 * n, :])
        st[0:3, :] += sums

    done = copy(gi, gi_h, sem.at[12])
    done.start()
    done.wait()

    @pl.when(core == 1)
    def _():
        copy(gt, gt_h, sem.at[13]).wait()


def k_more(par, st0, image_h, t2x_h, bx_h, edgex_h, gi0_h, gi_h, st, texts, image, tail, gi, sem, *, cycle):
    core, row, _ = spot(cycle)
    n = image.shape[0]
    far = STEPS * n
    loads = [
        copy(t2x_h, texts.at[0:n], sem.at[0]),
        copy(image_h.at[0:n], image, sem.at[1]),
        copy(image_h.at[n : n + TAIL], tail, sem.at[2]),
        copy(gi0_h, gi, sem.at[3]),
    ]
    start(*loads)

    @pl.when(core == 1)
    def _():
        copy(bx_h, texts.at[n : 2 * n], sem.at[4]).start()

    @pl.when((row == 0) & (core == 0))
    def _():
        copy(edgex_h.at[0:n], texts.at[n : 2 * n], sem.at[4]).start()

    wait(*loads)
    rel = decode(tail[...], n)
    two = (row == 0) | (core == 1)

    @pl.when(two)
    def _():
        copy(t2x_h, texts.at[n : 2 * n], sem.at[4]).wait()
        row_i = rows(n, far + jnp.where(core == 0, n, 3 * n), n + jnp.where(core == 0, 0, far))
        low, sums = pair(par, texts[...], image[...], rel, row_i, True)
        st[0:3, :] = st0[0:3, :] + sums
        gi[...] += dot_tn(low, texts[...])

    @pl.when(jnp.logical_not(two))
    def _():
        low, sums = pair(par, texts[0:n, :], image[...], rel, rows(n, far + n), True)
        st[0:3, :] = st0[0:3, :] + sums
        gi[...] += dot_tn(low, texts[0:n, :])

    done = copy(gi, gi_h, sem.at[5])
    done.start()
    done.wait()


def k_tail(par, st0, home, g0, gi, st, *, cycle):
    core, _, _ = spot(cycle)
    n, d = gi.shape

    @pl.when(core == 0)
    def _():
        gi[...] = par[0] * (g0[...] + home[0:n, :].astype(jnp.float32))
        parts = home[n : n + TAIL, 0:n].astype(jnp.float32)
        st[...] = st0[0:3, :] + parts[0:3] + parts[3:6] + parts[6:9]

    @pl.when(core == 1)
    def _():
        gi[...] = par[0] * g0[...]
        st[...] = st0[0:3, :]


def on_device(image_emb, text_emb, labels, logit_params):
    n, d = image_emb.shape
    groups = lax.axis_size("grp")
    cycle = lax.axis_size("blk")
    half = cycle // 2
    last = half // 2 - 1
    tie = lax.optimization_barrier

    def row_of(k):
        return k % half // 2

    def inner(k):
        return 0 < row_of(k) < last

    def send(value, pairs):
        return lax.ppermute(value, AXES, pairs)

    def moves(dg, dk, keep=lambda k: True):
        return [
            (g * cycle + k, (g + dg) % groups * cycle + (k + dk) % cycle)
            for g in range(groups)
            for k in range(cycle)
            if keep(k)
        ]

    swap = moves(0, 1, lambda k: k % 2 == 0) + moves(0, -1, lambda k: k % 2 == 1)

    par = logit_params
    f32 = jax.ShapeDtypeStruct((n, d), jnp.float32)
    low = jax.ShapeDtypeStruct((n, d), jnp.bfloat16)
    full = jax.ShapeDtypeStruct((n + TAIL, d), jnp.bfloat16)
    stat = jax.ShapeDtypeStruct((8, n), jnp.float32)
    smem = pl.BlockSpec(memory_space=pltpu.SMEM)
    vmem = pl.BlockSpec(memory_space=pltpu.VMEM)
    hbm = pl.BlockSpec(memory_space=pl.ANY)

    def block(parts=1):
        return pltpu.VMEM((parts * n, d), jnp.bfloat16)

    def tails(parts=1):
        return pltpu.VMEM((parts * TAIL, d), jnp.bfloat16)

    total = pltpu.VMEM((n, d), jnp.float32)

    def call(body, params, small, big, outs, out_specs, scratch, sems, units, alias=None):
        return pl.pallas_call(
            functools.partial(body, cycle=cycle),
            out_shape=outs,
            in_specs=[smem] * len(params) + [vmem] * len(small) + [hbm] * len(big),
            out_specs=out_specs,
            scratch_shapes=[*scratch, pltpu.SemaphoreType.DMA((sems,))] if sems else [],
            input_output_aliases=alias or {},
            compiler_params=pltpu.CompilerParams(vmem_limit_bytes=24 * 1024 * 1024),
            cost_estimate=pl.CostEstimate(flops=units, bytes_accessed=units, transcendentals=0),
        )(*params, *small, *big)

    def ahead(k):
        return row_of(k) == last and k % 2 == 0

    def behind(k):
        return row_of(k) == last and k % 2 == 1

    t1 = send(text_emb, moves(0, 2, lambda k: not behind(k)))
    b_in = send(text_emb, moves(1, 0, inner))
    early = send(text_emb, moves(1, 2, ahead))
    image, other, leaves = call(
        functools.partial(k_pack, groups=groups), [], [labels], [image_emb, text_emb], [full] * 3, [hbm] * 3,
        [block(), block(), tails()], 8, 0,
    )
    i1 = send(image, moves(0, -2))
    other = send(other, swap)
    g_img, g_txt, stats = call(
        k_first, [par], [], [image, text_emb, other], [f32, f32, stat], [hbm, hbm, vmem],
        [block(), tails(), block(), block(), tails(), total, total], 7, 5,
    )
    t1, i1, b_in, early, leaves, text, image, g_img = tie((t1, i1, b_in, early, leaves, text_emb, image, g_img))

    b_out = send(text, moves(1, 0, lambda k: not inner(k)))
    mix = call(k_mix, [], [], [b_in, text], low, hbm, [block()], 2, 0)
    t2_mix = send(mix, moves(0, 2, inner) + moves(1, 2, behind))
    t2_over = send(t1, moves(1, 0, lambda k: row_of(k) == 1))
    t1x = send(t1, swap)
    i1x = send(i1, swap)
    i2 = send(i1, moves(0, -1, lambda k: k % 2 == 0 and k % half != 0))
    edge = send(leaves, moves(0, 2, behind) + moves(0, -3, lambda k: k % half == 2))
    g_img, g_txt, stats = call(
        k_second, [par], [stats], [image, text, t1, t1x, i1, i1x, g_img, g_txt], [f32, f32, stat], [hbm, hbm, vmem],
        [block(), tails(), block(), block(2), block(2), tails(2), total, total], 13, 8, {8: 0, 9: 1},
    )
    b_out, b_in, edge, t2_over, g_img, g_txt = tie((b_out, b_in, edge, t2_over, g_img, g_txt))
    cross, b0 = call(
        k_cross, [par], [], [b_in, b_out, image, other, i1, i1x, i2, edge], [low, low], [vmem, hbm],
        [block(), block(4), tails(4)], 10, 8,
    )
    back = send(cross, moves(-1, 0))
    t2_mix, t2_over, cross = tie((t2_mix, t2_over, cross))
    away, t2 = call(
        k_away, [par], [], [i1x, t1, edge, early, t2_over, t2_mix], [full, low], [hbm, hbm],
        [block(), tails(), block(2), pltpu.VMEM((n + TAIL, d), jnp.bfloat16)], 6, 4,
    )
    home = send(away, moves(0, 1, lambda k: k % 2 == 1))
    bx = send(b0, moves(0, 1, lambda k: k % 2 == 0))
    t2x = send(t2, swap)
    edgex = send(edge, moves(0, -1, lambda k: row_of(k) == 0 and k % 2 == 1))
    g_img, g_txt, stats = call(
        k_late, [par], [stats], [b0, t2, edge, image, text, i2, g_img, g_txt], [f32, f32, stat],
        [hbm, hbm, vmem], [block(3), block(), tails(), block(), block(), tails(), total, total], 14, 8, {8: 0, 9: 1},
    )
    grad_text = logit_params[0] * (g_txt + back.astype(jnp.float32))
    grad_text, t2x, edgex, bx = tie((grad_text, t2x, edgex, bx))
    g_img, stats = call(
        k_more, [par], [stats], [image, t2x, bx, edgex, g_img], [f32, stat], [hbm, vmem],
        [block(2), block(), tails(), total], 6, 0, {6: 0},
    )
    home, g_img = tie((home, g_img))
    grad_image, stats = call(
        k_tail, [par], [stats, home, g_img], [], [f32, jax.ShapeDtypeStruct((3, n), jnp.float32)], [vmem, vmem], [], 0, 0,
    )
    return grad_image, grad_text, stats


def solution(mesh):
    return jax.shard_map(
        on_device,
        mesh=mesh,
        in_specs=(P(AXES, None), P(AXES, None), P(AXES), P()),
        out_specs=(P(AXES, None), P(AXES, None), P(None, AXES)),
        check_vma=False,
    )
```

```python
import functools

import jax
import jax.numpy as jnp
from jax import lax
from jax.experimental import pallas as pl
from jax.experimental.pallas import tpu as pltpu
from jax.sharding import PartitionSpec as P

STEPS = 4
AXES = ("grp", "blk")
TAIL = 16


def dot_nt(a, b):
    return lax.dot_general(a, b, (((1,), (1,)), ((), ())), preferred_element_type=jnp.float32)


def dot_nn(a, b):
    return lax.dot_general(a, b, (((1,), (0,)), ((), ())), preferred_element_type=jnp.float32)


def dot_tn(a, b):
    return lax.dot_general(a, b, (((0,), (0,)), ((), ())), preferred_element_type=jnp.float32)


def spot(cycle):
    place = lax.axis_index("blk")
    return lax.rem(place, 2), lax.div(lax.rem(place, cycle // 2), 2), cycle // 4 - 1


def decode(tail, n):
    codes = tail[:, 0:n].astype(jnp.float32)
    return codes[0:1, :] * 64.0 + codes[1:2, :]


def pair(par, texts, images, rel, row, want_stats):
    scale, bias = par[0], par[1]
    raw = dot_nt(texts, images)
    z = scale * raw + bias
    pos = rel == row
    e = jnp.exp(-jnp.abs(z))
    part = 1.0 / (1.0 + e)
    sig = jnp.where(z >= 0.0, part, e * part)
    grad = jnp.where(pos, sig - 1.0, sig)
    low = grad.astype(jnp.bfloat16)
    if not want_stats:
        return low, None
    loss = jnp.maximum(jnp.where(pos, -z, z), 0.0) + jnp.log1p(e)
    sums = [jnp.sum(v, axis=0, keepdims=True) for v in (loss, grad, grad * raw)]
    return low, jnp.concatenate(sums, axis=0)


def rows(n, *bases):
    one = lax.broadcasted_iota(jnp.int32, (n, 1), 0)
    return jnp.concatenate([one + b for b in bases], axis=0).astype(jnp.float32)


def copy(source, target, sem):
    return pltpu.make_async_copy(source, target, sem)


def start(*copies):
    for c in copies:
        c.start()


def wait(*copies):
    for c in copies:
        c.wait()


def k_pack(label, image_h, text_h, full_h, other_h, out_h, image, text, code, sem, *, cycle, groups):
    core, row, _ = spot(cycle)
    n = image.shape[0]
    load_i, load_t = copy(image_h, image, sem.at[0]), copy(text_h, text, sem.at[1])
    start(load_i, load_t)
    here = label[...].reshape(1, n)
    owner = lax.div(here, n)
    rnd = lax.rem(lax.axis_index("grp") - lax.div(owner, cycle) + groups, groups)
    step = lax.rem(lax.axis_index("blk") - lax.rem(owner, cycle) + cycle, cycle)
    rel = rnd * (STEPS * n) + step * n + lax.rem(here, n)
    code[...] = jnp.zeros(code.shape, jnp.bfloat16)
    fill = jnp.zeros((TAIL - 2, n), jnp.float32)
    parts = [lax.div(rel, 64).astype(jnp.float32), lax.rem(rel, 64).astype(jnp.float32), fill]
    code[:, 0:n] = jnp.concatenate(parts, axis=0).astype(jnp.bfloat16)
    marks = [copy(code, t.at[n : n + TAIL], sem.at[q + 2]) for q, t in enumerate((full_h, other_h, out_h))]
    start(*marks)
    wait(load_i, load_t)
    whole = copy(image, full_h.at[0:n], sem.at[5])
    whole.start()

    @pl.when(core == 0)
    def _():
        copy(text, other_h.at[0:n], sem.at[6]).start()

    @pl.when(core == 1)
    def _():
        copy(image, other_h.at[0:n], sem.at[6]).start()

    @pl.when((core == 0) & (row == 1))
    def _():
        copy(image, out_h.at[0:n], sem.at[7]).start()

    @pl.when((core == 1) | (row != 1))
    def _():
        copy(text, out_h.at[0:n], sem.at[7]).start()

    wait(*marks, whole)
    copy(text, other_h.at[0:n], sem.at[6]).wait()
    copy(text, out_h.at[0:n], sem.at[7]).wait()


def k_mix(inner_h, text_h, out_h, hold, sem, *, cycle):
    _, row, last = spot(cycle)

    @pl.when(row != last)
    def _():
        copy(inner_h, hold, sem.at[0]).start()

    @pl.when(row == last)
    def _():
        copy(text_h, hold, sem.at[0]).start()

    copy(inner_h, hold, sem.at[0]).wait()
    out = copy(hold, out_h, sem.at[1])
    out.start()
    out.wait()


def k_first(par, image_h, text_h, other_h, gi_h, gt_h, st, image, tail, text, extra, etail, gi, gt, sem, *, cycle):
    core, _, _ = spot(cycle)
    n = text.shape[0]
    loads = [
        copy(image_h.at[0:n], image, sem.at[0]),
        copy(image_h.at[n : n + TAIL], tail, sem.at[1]),
        copy(text_h, text, sem.at[2]),
        copy(other_h.at[0:n], extra, sem.at[3]),
        copy(other_h.at[n : n + TAIL], etail, sem.at[4]),
    ]
    start(*loads)
    wait(*loads[0:3])
    rel = decode(tail[...], n)
    low, sums = pair(par, text[...], image[...], rel, rows(n, 0), True)
    gt[...] = dot_nn(low, image[...])
    gi[...] = dot_tn(low, text[...])
    st[0:3, :] = sums
    wait(*loads[3:])

    @pl.when(core == 1)
    def _():
        low, sums = pair(par, extra[...], image[...], rel, rows(n, n), True)
        gi[...] += dot_tn(low, extra[...])
        st[0:3, :] += sums

    @pl.when(core == 0)
    def _():
        low, _ = pair(par, text[...], extra[...], decode(etail[...], n), rows(n, n), False)
        gt[...] += dot_nn(low, extra[...])

    out = [copy(gi, gi_h, sem.at[5]), copy(gt, gt_h, sem.at[6])]
    start(*out)
    wait(*out)


def k_second(
    par, st0, image_h, text_h, t1_h, t1x_h, i1_h, i1x_h, gi0_h, gt0_h, gi_h, gt_h, st,
    image, tail, text, texts, images, tails, gi, gt, sem, *, cycle,
):
    core, row, _ = spot(cycle)
    n = text.shape[0]
    near = core == 0
    loads = [
        copy(image_h.at[0:n], image, sem.at[0]),
        copy(image_h.at[n : n + TAIL], tail, sem.at[1]),
        copy(gi0_h, gi, sem.at[4]),
    ]

    @pl.when((row > 0) | near)
    def _():
        copy(t1_h, texts.at[0:n], sem.at[2]).start()

    @pl.when((row == 0) & (core == 1))
    def _():
        copy(t1x_h, texts.at[0:n], sem.at[2]).start()

    @pl.when(row > 0)
    def _():
        copy(t1x_h, texts.at[n : 2 * n], sem.at[3]).start()

    more = [
        copy(text_h, text, sem.at[5]),
        copy(i1_h.at[0:n], images.at[0:n], sem.at[6]),
        copy(i1_h.at[n : n + TAIL], tails.at[0:TAIL], sem.at[7]),
        copy(i1x_h.at[0:n], images.at[n : 2 * n], sem.at[8]),
        copy(i1x_h.at[n : n + TAIL], tails.at[TAIL : 2 * TAIL], sem.at[9]),
        copy(gt0_h, gt, sem.at[10]),
    ]
    out_i = copy(gi, gi_h, sem.at[11])
    start(*loads, *more)
    wait(*loads)
    copy(t1_h, texts.at[0:n], sem.at[2]).wait()

    @pl.when(row > 0)
    def _():
        copy(t1x_h, texts.at[n : 2 * n], sem.at[3]).wait()
        row_i = rows(n, 2 * n, jnp.where(near, n, 3 * n))
        low, sums = pair(par, texts[...], image[...], decode(tail[...], n), row_i, True)
        gi[...] += dot_tn(low, texts[...])
        st[0:3, :] = st0[0:3, :] + sums

    @pl.when(row == 0)
    def _():
        row_i = rows(n, jnp.where(near, 2 * n, 3 * n))
        low, sums = pair(par, texts[0:n, :], image[...], decode(tail[...], n), row_i, True)
        gi[...] += dot_tn(low, texts[0:n, :])
        st[0:3, :] = st0[0:3, :] + sums

    out_i.start()
    wait(*more)
    rel = jnp.concatenate(
        [
            decode(tails[0:TAIL, :], n) - jnp.float32(2 * n),
            decode(tails[TAIL : 2 * TAIL, :], n) - jnp.where(near, 3 * n, n).astype(jnp.float32),
        ],
        axis=1,
    )
    low, _ = pair(par, text[...], images[...], rel, rows(n, 0), False)
    gt[...] += dot_nn(low, images[...])
    out_t = copy(gt, gt_h, sem.at[12])
    out_t.start()
    wait(out_i, out_t)


def k_cross(
    par, inner_h, out_h, image_h, other_h, i1_h, i1x_h, i2_h, iw_h, out, b0_h,
    text, images, tails, sem, *, cycle,
):
    core, row, last = spot(cycle)
    n = text.shape[0]
    near = core == 0

    def part(source, q):
        return (
            copy(source.at[0:n], images.at[q * n : (q + 1) * n], sem.at[2 * q]),
            copy(source.at[n : n + TAIL], tails.at[q * TAIL : (q + 1) * TAIL], sem.at[2 * q + 1]),
        )

    late = (row == 0) | ((row == last) & (core == 0))

    @pl.when(late)
    def _():
        copy(out_h, text, sem.at[8]).start()

    @pl.when(jnp.logical_not(late))
    def _():
        copy(inner_h, text, sem.at[8]).start()

    for q, source in enumerate((image_h, i1_h, i1x_h)):
        start(*part(source, q))

    @pl.when(near)
    def _():
        start(*part(other_h, 3))

    @pl.when((core == 1) & (row != last))
    def _():
        start(*part(i2_h, 3))

    @pl.when((core == 1) & (row == last))
    def _():
        start(*part(iw_h, 3))

    copy(inner_h, text, sem.at[8]).wait()
    keep = copy(text, b0_h, sem.at[9])
    keep.start()
    for q in range(4):
        wait(*part(image_h, q))
    steps = (0, 2 * n, jnp.where(near, 3 * n, n), jnp.where(near, n, 3 * n))
    rel = [
        decode(tails[q * TAIL : (q + 1) * TAIL, :], n) - jnp.asarray(s + STEPS * n, jnp.float32)
        for q, s in enumerate(steps)
    ]
    row_t = rows(n, 0)
    first, _ = pair(par, text[...], images[0 : 2 * n, :], jnp.concatenate(rel[0:2], axis=1), row_t, False)
    second, _ = pair(par, text[...], images[2 * n : 4 * n, :], jnp.concatenate(rel[2:4], axis=1), row_t, False)
    out[...] = dot_nn(jnp.concatenate([first, second], axis=1), images[...]).astype(jnp.bfloat16)
    keep.wait()


def k_away(par, image_h, t1_h, edge_h, early_h, over_h, mix_h, out_h, t2_h, image, tail, texts, out, sem, *, cycle):
    core, row, _ = spot(cycle)
    n = t1_h.shape[0]
    first, second = texts.at[0:n], texts.at[n : 2 * n]

    @pl.when(row == 1)
    def _():
        copy(over_h, second, sem.at[0]).start()

    @pl.when((row == 0) & (core == 0))
    def _():
        copy(early_h, second, sem.at[0]).start()

    @pl.when((row > 1) | ((row == 0) & (core == 1)))
    def _():
        copy(mix_h, second, sem.at[0]).start()

    @pl.when(row == 0)
    def _():
        copy(edge_h.at[0:n], first, sem.at[3]).start()

    @pl.when(row != 0)
    def _():
        copy(t1_h, first, sem.at[3]).start()

    loads = [copy(image_h.at[0:n], image, sem.at[1]), copy(image_h.at[n : n + TAIL], tail, sem.at[2])]
    start(*loads)
    copy(mix_h, second, sem.at[0]).wait()
    keep = copy(second, t2_h, sem.at[4])
    keep.start()
    copy(t1_h, first, sem.at[3]).wait()
    wait(*loads)

    @pl.when(core == 1)
    def _():
        row_i = rows(n, 3 * n, (STEPS + 3) * n)
        low, sums = pair(par, texts[...], image[...], decode(tail[...], n), row_i, True)
        out[0:n, :] = dot_tn(low, texts[...]).astype(jnp.bfloat16)
        high = sums.astype(jnp.bfloat16)
        rest = sums - high.astype(jnp.float32)
        mid = rest.astype(jnp.bfloat16)
        end = (rest - mid.astype(jnp.float32)).astype(jnp.bfloat16)
        fill = jnp.zeros((TAIL - 9, n), jnp.bfloat16)
        out[n : n + TAIL, :] = jnp.zeros((TAIL, out.shape[1]), jnp.bfloat16)
        out[n : n + TAIL, 0:n] = jnp.concatenate([high, mid, end, fill], axis=0)
        done = copy(out, out_h, sem.at[5])
        done.start()
        done.wait()

    keep.wait()


def k_late(
    par, st0, b0_h, t2_h, edge_h, image_h, text_h, i2_h, gi0_h, gt0_h, gi_h, gt_h, st,
    texts, image, tail, text, extra, etail, gi, gt, sem, *, cycle,
):
    core, row, last = spot(cycle)
    n = text.shape[0]
    far = STEPS * n
    loads = [
        copy(b0_h, texts.at[0:n], sem.at[0]),
        copy(t2_h, texts.at[n : 2 * n], sem.at[1]),
        copy(image_h.at[0:n], image, sem.at[3]),
        copy(image_h.at[n : n + TAIL], tail, sem.at[4]),
        copy(gi0_h, gi, sem.at[5]),
    ]
    start(*loads)

    @pl.when(core == 1)
    def _():
        start(copy(text_h, text, sem.at[7]), copy(gt0_h, gt, sem.at[8]))

    @pl.when((core == 1) & (row != last))
    def _():
        start(copy(i2_h.at[0:n], extra, sem.at[9]), copy(i2_h.at[n : n + TAIL], etail, sem.at[10]))

    @pl.when((core == 1) & (row == last))
    def _():
        start(copy(edge_h.at[0:n], extra, sem.at[9]), copy(edge_h.at[n : n + TAIL], etail, sem.at[10]))

    @pl.when((row == 0) & (core == 1))
    def _():
        copy(edge_h.at[0:n], texts.at[2 * n : 3 * n], sem.at[11]).start()

    wait(*loads[0:4])
    rel = decode(tail[...], n)
    low, sums = pair(par, texts[0 : 2 * n, :], image[...], rel, rows(n, far, far + 2 * n), True)
    loads[4].wait()
    gi[...] += dot_tn(low, texts[0 : 2 * n, :])
    st[0:3, :] = st0[0:3, :] + sums

    @pl.when(core == 1)
    def _():
        wait(copy(text_h, text, sem.at[7]), copy(gt0_h, gt, sem.at[8]))
        wait(copy(i2_h.at[0:n], extra, sem.at[9]), copy(i2_h.at[n : n + TAIL], etail, sem.at[10]))
        low, _ = pair(par, text[...], extra[...], decode(etail[...], n), rows(n, 3 * n), False)
        gt[...] += dot_nn(low, extra[...])
        copy(gt, gt_h, sem.at[13]).start()

    @pl.when((row == 0) & (core == 1))
    def _():
        copy(edge_h.at[0:n], texts.at[2 * n : 3 * n], sem.at[11]).wait()
        low, sums = pair(par, texts[2 * n : 3 * n, :], image[...], rel, rows(n, 2 * n), True)
        gi[...] += dot_tn(low, texts[2 * n : 3 * n, :])
        st[0:3, :] += sums

    done = copy(gi, gi_h, sem.at[12])
    done.start()
    done.wait()

    @pl.when(core == 1)
    def _():
        copy(gt, gt_h, sem.at[13]).wait()


def k_more(par, st0, image_h, t2x_h, bx_h, edgex_h, gi0_h, gi_h, st, texts, image, tail, gi, sem, *, cycle):
    core, row, _ = spot(cycle)
    n = image.shape[0]
    far = STEPS * n
    loads = [
        copy(t2x_h, texts.at[0:n], sem.at[0]),
        copy(image_h.at[0:n], image, sem.at[1]),
        copy(image_h.at[n : n + TAIL], tail, sem.at[2]),
        copy(gi0_h, gi, sem.at[3]),
    ]
    start(*loads)

    @pl.when(core == 1)
    def _():
        copy(bx_h, texts.at[n : 2 * n], sem.at[4]).start()

    @pl.when((row == 0) & (core == 0))
    def _():
        copy(edgex_h.at[0:n], texts.at[n : 2 * n], sem.at[4]).start()

    wait(*loads)
    rel = decode(tail[...], n)
    two = (row == 0) | (core == 1)

    @pl.when(two)
    def _():
        copy(t2x_h, texts.at[n : 2 * n], sem.at[4]).wait()
        row_i = rows(n, far + jnp.where(core == 0, n, 3 * n), n + jnp.where(core == 0, 0, far))
        low, sums = pair(par, texts[...], image[...], rel, row_i, True)
        st[0:3, :] = st0[0:3, :] + sums
        gi[...] += dot_tn(low, texts[...])

    @pl.when(jnp.logical_not(two))
    def _():
        low, sums = pair(par, texts[0:n, :], image[...], rel, rows(n, far + n), True)
        st[0:3, :] = st0[0:3, :] + sums
        gi[...] += dot_tn(low, texts[0:n, :])

    done = copy(gi, gi_h, sem.at[5])
    done.start()
    done.wait()


def k_tail(par, st0, home, g0, gi, st, *, cycle):
    core, _, _ = spot(cycle)
    n, d = gi.shape

    @pl.when(core == 0)
    def _():
        gi[...] = par[0] * (g0[...] + home[0:n, :].astype(jnp.float32))
        parts = home[n : n + TAIL, 0:n].astype(jnp.float32)
        st[...] = st0[0:3, :] + parts[0:3] + parts[3:6] + parts[6:9]

    @pl.when(core == 1)
    def _():
        gi[...] = par[0] * g0[...]
        st[...] = st0[0:3, :]


def on_device(image_emb, text_emb, labels, logit_params):
    n, d = image_emb.shape
    groups = lax.axis_size("grp")
    cycle = lax.axis_size("blk")
    half = cycle // 2
    last = half // 2 - 1
    tie = lax.optimization_barrier

    def row_of(k):
        return k % half // 2

    def inner(k):
        return 0 < row_of(k) < last

    def send(value, pairs):
        return lax.ppermute(value, AXES, pairs)

    def moves(dg, dk, keep=lambda k: True):
        return [
            (g * cycle + k, (g + dg) % groups * cycle + (k + dk) % cycle)
            for g in range(groups)
            for k in range(cycle)
            if keep(k)
        ]

    swap = moves(0, 1, lambda k: k % 2 == 0) + moves(0, -1, lambda k: k % 2 == 1)

    par = logit_params
    f32 = jax.ShapeDtypeStruct((n, d), jnp.float32)
    low = jax.ShapeDtypeStruct((n, d), jnp.bfloat16)
    full = jax.ShapeDtypeStruct((n + TAIL, d), jnp.bfloat16)
    stat = jax.ShapeDtypeStruct((8, n), jnp.float32)
    smem = pl.BlockSpec(memory_space=pltpu.SMEM)
    vmem = pl.BlockSpec(memory_space=pltpu.VMEM)
    hbm = pl.BlockSpec(memory_space=pl.ANY)

    def block(parts=1):
        return pltpu.VMEM((parts * n, d), jnp.bfloat16)

    def tails(parts=1):
        return pltpu.VMEM((parts * TAIL, d), jnp.bfloat16)

    total = pltpu.VMEM((n, d), jnp.float32)

    def call(body, params, small, big, outs, out_specs, scratch, sems, units, alias=None):
        return pl.pallas_call(
            functools.partial(body, cycle=cycle),
            out_shape=outs,
            in_specs=[smem] * len(params) + [vmem] * len(small) + [hbm] * len(big),
            out_specs=out_specs,
            scratch_shapes=[*scratch, pltpu.SemaphoreType.DMA((sems,))] if sems else [],
            input_output_aliases=alias or {},
            compiler_params=pltpu.CompilerParams(vmem_limit_bytes=24 * 1024 * 1024),
            cost_estimate=pl.CostEstimate(flops=units, bytes_accessed=units, transcendentals=0),
        )(*params, *small, *big)

    def ahead(k):
        return row_of(k) == last and k % 2 == 0

    def behind(k):
        return row_of(k) == last and k % 2 == 1

    t1 = send(text_emb, moves(0, 2, lambda k: not behind(k)))
    b_in = send(text_emb, moves(1, 0, lambda k: inner(k) or behind(k)))
    early = send(text_emb, moves(1, 2, ahead))
    image, other, leaves = call(
        functools.partial(k_pack, groups=groups), [], [labels], [image_emb, text_emb], [full] * 3, [hbm] * 3,
        [block(), block(), tails()], 8, 0,
    )
    i1 = send(image, moves(0, -2))
    other = send(other, swap)
    g_img, g_txt, stats = call(
        k_first, [par], [], [image, text_emb, other], [f32, f32, stat], [hbm, hbm, vmem],
        [block(), tails(), block(), block(), tails(), total, total], 7, 5,
    )
    t1, i1, b_in, early, leaves, text, image, g_img = tie((t1, i1, b_in, early, leaves, text_emb, image, g_img))

    b_out = send(text, moves(1, 0, lambda k: row_of(k) == 0 or ahead(k)))
    mix = call(k_mix, [], [], [b_in, text], low, hbm, [block()], 2, 0)
    t2_mix = send(mix, moves(0, 2, inner) + moves(1, 2, behind))
    t2_over = send(t1, moves(1, 0, lambda k: row_of(k) == 1))
    t1x = send(t1, swap)
    i1x = send(i1, swap)
    i2 = send(i1, moves(0, -1, lambda k: k % 2 == 0 and k % half != 0))
    edge = send(leaves, moves(0, 2, behind) + moves(0, -3, lambda k: k % half == 2))
    g_img, g_txt, stats = call(
        k_second, [par], [stats], [image, text, t1, t1x, i1, i1x, g_img, g_txt], [f32, f32, stat], [hbm, hbm, vmem],
        [block(), tails(), block(), block(2), block(2), tails(2), total, total], 13, 8, {8: 0, 9: 1},
    )
    b_out, b_in, edge, t2_over, g_img, g_txt = tie((b_out, b_in, edge, t2_over, g_img, g_txt))
    cross, b0 = call(
        k_cross, [par], [], [b_in, b_out, image, other, i1, i1x, i2, edge], [low, low], [vmem, hbm],
        [block(), block(4), tails(4)], 10, 8,
    )
    back = send(cross, moves(-1, 0))
    t2_mix, t2_over, cross = tie((t2_mix, t2_over, cross))
    away, t2 = call(
        k_away, [par], [], [i1x, t1, edge, early, t2_over, t2_mix], [full, low], [hbm, hbm],
        [block(), tails(), block(2), pltpu.VMEM((n + TAIL, d), jnp.bfloat16)], 6, 4,
    )
    home = send(away, moves(0, 1, lambda k: k % 2 == 1))
    bx = send(b0, moves(0, 1, lambda k: k % 2 == 0))
    t2x = send(t2, swap)
    edgex = send(edge, moves(0, -1, lambda k: row_of(k) == 0 and k % 2 == 1))
    g_img, g_txt, stats = call(
        k_late, [par], [stats], [b0, t2, edge, image, text, i2, g_img, g_txt], [f32, f32, stat],
        [hbm, hbm, vmem], [block(3), block(), tails(), block(), block(), tails(), total, total], 14, 8, {8: 0, 9: 1},
    )
    grad_text = logit_params[0] * (g_txt + back.astype(jnp.float32))
    grad_text, t2x, edgex, bx = tie((grad_text, t2x, edgex, bx))
    g_img, stats = call(
        k_more, [par], [stats], [image, t2x, bx, edgex, g_img], [f32, stat], [hbm, vmem],
        [block(2), block(), tails(), total], 6, 0, {6: 0},
    )
    home, g_img = tie((home, g_img))
    grad_image, stats = call(
        k_tail, [par], [stats, home, g_img], [], [f32, jax.ShapeDtypeStruct((3, n), jnp.float32)], [vmem, vmem], [], 0, 0,
    )
    return grad_image, grad_text, stats


def solution(mesh):
    return jax.shard_map(
        on_device,
        mesh=mesh,
        in_specs=(P(AXES, None), P(AXES, None), P(AXES), P()),
        out_specs=(P(AXES, None), P(AXES, None), P(None, AXES)),
        check_vma=False,
    )
```

```python
import functools

import jax
import jax.numpy as jnp
from jax import lax
from jax.experimental import pallas as pl
from jax.experimental.pallas import tpu as pltpu
from jax.sharding import PartitionSpec as P

STEPS = 4
AXES = ("grp", "blk")
TAIL = 16


def dot_nt(a, b):
    return lax.dot_general(a, b, (((1,), (1,)), ((), ())), preferred_element_type=jnp.float32)


def dot_nn(a, b):
    return lax.dot_general(a, b, (((1,), (0,)), ((), ())), preferred_element_type=jnp.float32)


def dot_tn(a, b):
    return lax.dot_general(a, b, (((0,), (0,)), ((), ())), preferred_element_type=jnp.float32)


def spot(cycle):
    place = lax.axis_index("blk")
    return lax.rem(place, 2), lax.div(lax.rem(place, cycle // 2), 2), cycle // 4 - 1


def decode(tail, n):
    codes = tail[:, 0:n].astype(jnp.float32)
    return codes[0:1, :] * 64.0 + codes[1:2, :]


def pair(par, texts, images, rel, row, want_stats):
    scale, bias = par[0], par[1]
    raw = dot_nt(texts, images)
    z = scale * raw + bias
    pos = rel == row
    e = jnp.exp(-jnp.abs(z))
    part = 1.0 / (1.0 + e)
    sig = jnp.where(z >= 0.0, part, e * part)
    grad = jnp.where(pos, sig - 1.0, sig)
    low = grad.astype(jnp.bfloat16)
    if not want_stats:
        return low, None
    loss = jnp.maximum(jnp.where(pos, -z, z), 0.0) + jnp.log1p(e)
    sums = [jnp.sum(v, axis=0, keepdims=True) for v in (loss, grad, grad * raw)]
    return low, jnp.concatenate(sums, axis=0)


def rows(n, *bases):
    one = lax.broadcasted_iota(jnp.int32, (n, 1), 0)
    return jnp.concatenate([one + b for b in bases], axis=0).astype(jnp.float32)


def copy(source, target, sem):
    return pltpu.make_async_copy(source, target, sem)


def start(*copies):
    for c in copies:
        c.start()


def wait(*copies):
    for c in copies:
        c.wait()


def k_pack(label, image_h, text_h, full_h, other_h, out_h, image, text, code, sem, *, cycle, groups):
    core, row, _ = spot(cycle)
    n = image.shape[0]
    load_i, load_t = copy(image_h, image, sem.at[0]), copy(text_h, text, sem.at[1])
    start(load_i, load_t)
    here = label[...].reshape(1, n)
    owner = lax.div(here, n)
    rnd = lax.rem(lax.axis_index("grp") - lax.div(owner, cycle) + groups, groups)
    step = lax.rem(lax.axis_index("blk") - lax.rem(owner, cycle) + cycle, cycle)
    rel = rnd * (STEPS * n) + step * n + lax.rem(here, n)
    code[...] = jnp.zeros(code.shape, jnp.bfloat16)
    fill = jnp.zeros((TAIL - 2, n), jnp.float32)
    parts = [lax.div(rel, 64).astype(jnp.float32), lax.rem(rel, 64).astype(jnp.float32), fill]
    code[:, 0:n] = jnp.concatenate(parts, axis=0).astype(jnp.bfloat16)
    marks = [copy(code, t.at[n : n + TAIL], sem.at[q + 2]) for q, t in enumerate((full_h, other_h, out_h))]
    start(*marks)
    wait(load_i, load_t)
    whole = copy(image, full_h.at[0:n], sem.at[5])
    whole.start()

    @pl.when(core == 0)
    def _():
        copy(text, other_h.at[0:n], sem.at[6]).start()

    @pl.when(core == 1)
    def _():
        copy(image, other_h.at[0:n], sem.at[6]).start()

    @pl.when((core == 0) & (row == 1))
    def _():
        copy(image, out_h.at[0:n], sem.at[7]).start()

    @pl.when((core == 1) | (row != 1))
    def _():
        copy(text, out_h.at[0:n], sem.at[7]).start()

    wait(*marks, whole)
    copy(text, other_h.at[0:n], sem.at[6]).wait()
    copy(text, out_h.at[0:n], sem.at[7]).wait()


def k_mix(inner_h, text_h, out_h, hold, sem, *, cycle):
    _, row, last = spot(cycle)

    @pl.when(row != last)
    def _():
        copy(inner_h, hold, sem.at[0]).start()

    @pl.when(row == last)
    def _():
        copy(text_h, hold, sem.at[0]).start()

    copy(inner_h, hold, sem.at[0]).wait()
    out = copy(hold, out_h, sem.at[1])
    out.start()
    out.wait()


def k_first(par, image_h, text_h, other_h, gi_h, gt_h, st, image, tail, text, extra, etail, gi, gt, sem, *, cycle):
    core, _, _ = spot(cycle)
    n = text.shape[0]
    loads = [
        copy(image_h.at[0:n], image, sem.at[0]),
        copy(image_h.at[n : n + TAIL], tail, sem.at[1]),
        copy(text_h, text, sem.at[2]),
        copy(other_h.at[0:n], extra, sem.at[3]),
        copy(other_h.at[n : n + TAIL], etail, sem.at[4]),
    ]
    start(*loads)
    wait(*loads[0:3])
    rel = decode(tail[...], n)
    low, sums = pair(par, text[...], image[...], rel, rows(n, 0), True)
    gt[...] = dot_nn(low, image[...])
    gi[...] = dot_tn(low, text[...])
    st[0:3, :] = sums
    wait(*loads[3:])

    @pl.when(core == 1)
    def _():
        low, sums = pair(par, extra[...], image[...], rel, rows(n, n), True)
        gi[...] += dot_tn(low, extra[...])
        st[0:3, :] += sums

    @pl.when(core == 0)
    def _():
        low, _ = pair(par, text[...], extra[...], decode(etail[...], n), rows(n, n), False)
        gt[...] += dot_nn(low, extra[...])

    out = [copy(gi, gi_h, sem.at[5]), copy(gt, gt_h, sem.at[6])]
    start(*out)
    wait(*out)


def k_second(
    par, st0, image_h, text_h, t1_h, t1x_h, i1_h, i1x_h, gi0_h, gt0_h, gi_h, gt_h, st,
    image, tail, text, texts, images, tails, gi, gt, sem, *, cycle,
):
    core, row, _ = spot(cycle)
    n = text.shape[0]
    near = core == 0
    loads = [
        copy(image_h.at[0:n], image, sem.at[0]),
        copy(image_h.at[n : n + TAIL], tail, sem.at[1]),
        copy(gi0_h, gi, sem.at[4]),
    ]

    @pl.when((row > 0) | near)
    def _():
        copy(t1_h, texts.at[0:n], sem.at[2]).start()

    @pl.when((row == 0) & (core == 1))
    def _():
        copy(t1x_h, texts.at[0:n], sem.at[2]).start()

    @pl.when(row > 0)
    def _():
        copy(t1x_h, texts.at[n : 2 * n], sem.at[3]).start()

    more = [
        copy(text_h, text, sem.at[5]),
        copy(i1_h.at[0:n], images.at[0:n], sem.at[6]),
        copy(i1_h.at[n : n + TAIL], tails.at[0:TAIL], sem.at[7]),
        copy(i1x_h.at[0:n], images.at[n : 2 * n], sem.at[8]),
        copy(i1x_h.at[n : n + TAIL], tails.at[TAIL : 2 * TAIL], sem.at[9]),
        copy(gt0_h, gt, sem.at[10]),
    ]
    out_i = copy(gi, gi_h, sem.at[11])
    start(*loads, *more)
    wait(*loads)
    copy(t1_h, texts.at[0:n], sem.at[2]).wait()

    @pl.when(row > 0)
    def _():
        copy(t1x_h, texts.at[n : 2 * n], sem.at[3]).wait()
        row_i = rows(n, 2 * n, jnp.where(near, n, 3 * n))
        low, sums = pair(par, texts[...], image[...], decode(tail[...], n), row_i, True)
        gi[...] += dot_tn(low, texts[...])
        st[0:3, :] = st0[0:3, :] + sums

    @pl.when(row == 0)
    def _():
        row_i = rows(n, jnp.where(near, 2 * n, 3 * n))
        low, sums = pair(par, texts[0:n, :], image[...], decode(tail[...], n), row_i, True)
        gi[...] += dot_tn(low, texts[0:n, :])
        st[0:3, :] = st0[0:3, :] + sums

    out_i.start()
    wait(*more)
    rel = jnp.concatenate(
        [
            decode(tails[0:TAIL, :], n) - jnp.float32(2 * n),
            decode(tails[TAIL : 2 * TAIL, :], n) - jnp.where(near, 3 * n, n).astype(jnp.float32),
        ],
        axis=1,
    )
    low, _ = pair(par, text[...], images[...], rel, rows(n, 0), False)
    gt[...] += dot_nn(low, images[...])
    out_t = copy(gt, gt_h, sem.at[12])
    out_t.start()
    wait(out_i, out_t)


def k_cross(
    par, inner_h, out_h, image_h, other_h, i1_h, i1x_h, i2_h, iw_h, own_h, gt0_h, out, b0_h, gt_h,
    text, images, tails, own, gt, sem, *, cycle,
):
    core, row, last = spot(cycle)
    n = text.shape[0]
    near = core == 0

    def part(source, q):
        return (
            copy(source.at[0:n], images.at[q * n : (q + 1) * n], sem.at[2 * q]),
            copy(source.at[n : n + TAIL], tails.at[q * TAIL : (q + 1) * TAIL], sem.at[2 * q + 1]),
        )

    late = (row == 0) | ((row == last) & (core == 0))

    @pl.when(late)
    def _():
        copy(out_h, text, sem.at[8]).start()

    @pl.when(jnp.logical_not(late))
    def _():
        copy(inner_h, text, sem.at[8]).start()

    for q, source in enumerate((image_h, i1_h, i1x_h)):
        start(*part(source, q))

    @pl.when(near)
    def _():
        start(*part(other_h, 3))

    @pl.when((core == 1) & (row != last))
    def _():
        start(*part(i2_h, 3))

    @pl.when((core == 1) & (row == last))
    def _():
        start(*part(iw_h, 3))

    @pl.when(core == 1)
    def _():
        start(copy(own_h, own, sem.at[10]), copy(gt0_h, gt, sem.at[11]))

    copy(inner_h, text, sem.at[8]).wait()
    keep = copy(text, b0_h, sem.at[9])
    keep.start()
    for q in range(4):
        wait(*part(image_h, q))
    steps = (0, 2 * n, jnp.where(near, 3 * n, n), jnp.where(near, n, 3 * n))
    rel = [
        decode(tails[q * TAIL : (q + 1) * TAIL, :], n) - jnp.asarray(s + STEPS * n, jnp.float32)
        for q, s in enumerate(steps)
    ]
    row_t = rows(n, 0)
    first, _ = pair(par, text[...], images[0 : 2 * n, :], jnp.concatenate(rel[0:2], axis=1), row_t, False)
    second, _ = pair(par, text[...], images[2 * n : 4 * n, :], jnp.concatenate(rel[2:4], axis=1), row_t, False)
    out[...] = dot_nn(jnp.concatenate([first, second], axis=1), images[...]).astype(jnp.bfloat16)

    @pl.when(core == 1)
    def _():
        wait(copy(own_h, own, sem.at[10]), copy(gt0_h, gt, sem.at[11]))
        mine = decode(tails[3 * TAIL : 4 * TAIL, :], n)
        low, _ = pair(par, own[...], images[3 * n : 4 * n, :], mine, rows(n, 3 * n), False)
        gt[...] += dot_nn(low, images[3 * n : 4 * n, :])
        done = copy(gt, gt_h, sem.at[12])
        done.start()
        done.wait()

    keep.wait()


def k_away(par, image_h, t1_h, edge_h, early_h, over_h, mix_h, out_h, t2_h, image, tail, texts, out, sem, *, cycle):
    core, row, _ = spot(cycle)
    n = t1_h.shape[0]
    first, second = texts.at[0:n], texts.at[n : 2 * n]

    @pl.when(row == 1)
    def _():
        copy(over_h, second, sem.at[0]).start()

    @pl.when((row == 0) & (core == 0))
    def _():
        copy(early_h, second, sem.at[0]).start()

    @pl.when((row > 1) | ((row == 0) & (core == 1)))
    def _():
        copy(mix_h, second, sem.at[0]).start()

    @pl.when(row == 0)
    def _():
        copy(edge_h.at[0:n], first, sem.at[3]).start()

    @pl.when(row != 0)
    def _():
        copy(t1_h, first, sem.at[3]).start()

    loads = [copy(image_h.at[0:n], image, sem.at[1]), copy(image_h.at[n : n + TAIL], tail, sem.at[2])]
    start(*loads)
    copy(mix_h, second, sem.at[0]).wait()
    keep = copy(second, t2_h, sem.at[4])
    keep.start()
    copy(t1_h, first, sem.at[3]).wait()
    wait(*loads)

    @pl.when(core == 1)
    def _():
        row_i = rows(n, 3 * n, (STEPS + 3) * n)
        low, sums = pair(par, texts[...], image[...], decode(tail[...], n), row_i, True)
        out[0:n, :] = dot_tn(low, texts[...]).astype(jnp.bfloat16)
        high = sums.astype(jnp.bfloat16)
        rest = sums - high.astype(jnp.float32)
        mid = rest.astype(jnp.bfloat16)
        end = (rest - mid.astype(jnp.float32)).astype(jnp.bfloat16)
        fill = jnp.zeros((TAIL - 9, n), jnp.bfloat16)
        out[n : n + TAIL, :] = jnp.zeros((TAIL, out.shape[1]), jnp.bfloat16)
        out[n : n + TAIL, 0:n] = jnp.concatenate([high, mid, end, fill], axis=0)
        done = copy(out, out_h, sem.at[5])
        done.start()
        done.wait()

    keep.wait()


def k_late(
    par, st0, b0_h, t2_h, edge_h, image_h, gi0_h, gi_h, st, texts, image, tail, gi, sem, *, cycle,
):
    core, row, _ = spot(cycle)
    n = image.shape[0]
    far = STEPS * n
    loads = [
        copy(b0_h, texts.at[0:n], sem.at[0]),
        copy(t2_h, texts.at[n : 2 * n], sem.at[1]),
        copy(image_h.at[0:n], image, sem.at[3]),
        copy(image_h.at[n : n + TAIL], tail, sem.at[4]),
        copy(gi0_h, gi, sem.at[5]),
    ]
    start(*loads)

    @pl.when((row == 0) & (core == 1))
    def _():
        copy(edge_h.at[0:n], texts.at[2 * n : 3 * n], sem.at[11]).start()

    wait(*loads[0:4])
    rel = decode(tail[...], n)

    @pl.when((row == 0) & (core == 1))
    def _():
        copy(edge_h.at[0:n], texts.at[2 * n : 3 * n], sem.at[11]).wait()
        low, sums = pair(par, texts[...], image[...], rel, rows(n, far, far + 2 * n, 2 * n), True)
        st[0:3, :] = st0[0:3, :] + sums
        loads[4].wait()
        gi[...] += dot_tn(low, texts[...])

    @pl.when((row != 0) | (core != 1))
    def _():
        low, sums = pair(par, texts[0 : 2 * n, :], image[...], rel, rows(n, far, far + 2 * n), True)
        st[0:3, :] = st0[0:3, :] + sums
        loads[4].wait()
        gi[...] += dot_tn(low, texts[0 : 2 * n, :])

    done = copy(gi, gi_h, sem.at[12])
    done.start()
    done.wait()


def k_more(par, st0, image_h, t2x_h, bx_h, edgex_h, gi0_h, gi_h, st, texts, image, tail, gi, sem, *, cycle):
    core, row, _ = spot(cycle)
    n = image.shape[0]
    far = STEPS * n
    loads = [
        copy(t2x_h, texts.at[0:n], sem.at[0]),
        copy(image_h.at[0:n], image, sem.at[1]),
        copy(image_h.at[n : n + TAIL], tail, sem.at[2]),
        copy(gi0_h, gi, sem.at[3]),
    ]
    start(*loads)

    @pl.when(core == 1)
    def _():
        copy(bx_h, texts.at[n : 2 * n], sem.at[4]).start()

    @pl.when((row == 0) & (core == 0))
    def _():
        copy(edgex_h.at[0:n], texts.at[n : 2 * n], sem.at[4]).start()

    wait(*loads[0:3])
    rel = decode(tail[...], n)
    two = (row == 0) | (core == 1)

    @pl.when(two)
    def _():
        copy(t2x_h, texts.at[n : 2 * n], sem.at[4]).wait()
        row_i = rows(n, far + jnp.where(core == 0, n, 3 * n), n + jnp.where(core == 0, 0, far))
        low, sums = pair(par, texts[...], image[...], rel, row_i, True)
        st[0:3, :] = st0[0:3, :] + sums
        loads[3].wait()
        gi[...] += dot_tn(low, texts[...])

    @pl.when(jnp.logical_not(two))
    def _():
        low, sums = pair(par, texts[0:n, :], image[...], rel, rows(n, far + n), True)
        st[0:3, :] = st0[0:3, :] + sums
        loads[3].wait()
        gi[...] += dot_tn(low, texts[0:n, :])

    done = copy(gi, gi_h, sem.at[5])
    done.start()
    done.wait()


def k_tail(par, st0, home, g0, gi, st, *, cycle):
    core, _, _ = spot(cycle)
    n, d = gi.shape

    @pl.when(core == 0)
    def _():
        gi[...] = par[0] * (g0[...] + home[0:n, :].astype(jnp.float32))
        parts = home[n : n + TAIL, 0:n].astype(jnp.float32)
        st[...] = st0[0:3, :] + parts[0:3] + parts[3:6] + parts[6:9]

    @pl.when(core == 1)
    def _():
        gi[...] = par[0] * g0[...]
        st[...] = st0[0:3, :]


def on_device(image_emb, text_emb, labels, logit_params):
    n, d = image_emb.shape
    groups = lax.axis_size("grp")
    cycle = lax.axis_size("blk")
    half = cycle // 2
    last = half // 2 - 1
    tie = lax.optimization_barrier

    def row_of(k):
        return k % half // 2

    def inner(k):
        return 0 < row_of(k) < last

    def send(value, pairs):
        return lax.ppermute(value, AXES, pairs)

    def moves(dg, dk, keep=lambda k: True):
        return [
            (g * cycle + k, (g + dg) % groups * cycle + (k + dk) % cycle)
            for g in range(groups)
            for k in range(cycle)
            if keep(k)
        ]

    swap = moves(0, 1, lambda k: k % 2 == 0) + moves(0, -1, lambda k: k % 2 == 1)

    par = logit_params
    f32 = jax.ShapeDtypeStruct((n, d), jnp.float32)
    low = jax.ShapeDtypeStruct((n, d), jnp.bfloat16)
    full = jax.ShapeDtypeStruct((n + TAIL, d), jnp.bfloat16)
    stat = jax.ShapeDtypeStruct((8, n), jnp.float32)
    smem = pl.BlockSpec(memory_space=pltpu.SMEM)
    vmem = pl.BlockSpec(memory_space=pltpu.VMEM)
    hbm = pl.BlockSpec(memory_space=pl.ANY)

    def block(parts=1):
        return pltpu.VMEM((parts * n, d), jnp.bfloat16)

    def tails(parts=1):
        return pltpu.VMEM((parts * TAIL, d), jnp.bfloat16)

    total = pltpu.VMEM((n, d), jnp.float32)

    def call(body, params, small, big, outs, out_specs, scratch, sems, units, alias=None):
        return pl.pallas_call(
            functools.partial(body, cycle=cycle),
            out_shape=outs,
            in_specs=[smem] * len(params) + [vmem] * len(small) + [hbm] * len(big),
            out_specs=out_specs,
            scratch_shapes=[*scratch, pltpu.SemaphoreType.DMA((sems,))] if sems else [],
            input_output_aliases=alias or {},
            compiler_params=pltpu.CompilerParams(vmem_limit_bytes=24 * 1024 * 1024),
            cost_estimate=pl.CostEstimate(flops=units, bytes_accessed=units, transcendentals=0),
        )(*params, *small, *big)

    def ahead(k):
        return row_of(k) == last and k % 2 == 0

    def behind(k):
        return row_of(k) == last and k % 2 == 1

    t1 = send(text_emb, moves(0, 2, lambda k: not behind(k)))
    b_in = send(text_emb, moves(1, 0, lambda k: inner(k) or behind(k)))
    early = send(text_emb, moves(1, 2, ahead))
    image, other, leaves = call(
        functools.partial(k_pack, groups=groups), [], [labels], [image_emb, text_emb], [full] * 3, [hbm] * 3,
        [block(), block(), tails()], 8, 0,
    )
    i1 = send(image, moves(0, -2))
    other = send(other, swap)
    g_img, g_txt, stats = call(
        k_first, [par], [], [image, text_emb, other], [f32, f32, stat], [hbm, hbm, vmem],
        [block(), tails(), block(), block(), tails(), total, total], 7, 5,
    )
    t1, i1, b_in, early, leaves, text, image, g_img = tie((t1, i1, b_in, early, leaves, text_emb, image, g_img))

    b_out = send(text, moves(1, 0, lambda k: row_of(k) == 0 or ahead(k)))
    mix = call(k_mix, [], [], [b_in, text], low, hbm, [block()], 2, 0)
    t2_mix = send(mix, moves(0, 2, inner) + moves(1, 2, behind))
    t2_over = send(t1, moves(1, 0, lambda k: row_of(k) == 1))
    t1x = send(t1, swap)
    i1x = send(i1, swap)
    i2 = send(i1, moves(0, -1, lambda k: k % 2 == 0 and k % half != 0))
    edge = send(leaves, moves(0, 2, behind) + moves(0, -3, lambda k: k % half == 2))
    g_img, g_txt, stats = call(
        k_second, [par], [stats], [image, text, t1, t1x, i1, i1x, g_img, g_txt], [f32, f32, stat], [hbm, hbm, vmem],
        [block(), tails(), block(), block(2), block(2), tails(2), total, total], 13, 8, {8: 0, 9: 1},
    )
    b_out, b_in, edge, t2_over, g_img, g_txt = tie((b_out, b_in, edge, t2_over, g_img, g_txt))
    cross, b0, g_txt = call(
        k_cross, [par], [], [b_in, b_out, image, other, i1, i1x, i2, edge, text, g_txt], [low, low, f32], [vmem, hbm, hbm],
        [block(), block(4), tails(4), block(), total], 13, 8, {10: 2},
    )
    back = send(cross, moves(-1, 0))
    t2_mix, t2_over, cross = tie((t2_mix, t2_over, cross))
    away, t2 = call(
        k_away, [par], [], [i1x, t1, edge, early, t2_over, t2_mix], [full, low], [hbm, hbm],
        [block(), tails(), block(2), pltpu.VMEM((n + TAIL, d), jnp.bfloat16)], 6, 4,
    )
    home = send(away, moves(0, 1, lambda k: k % 2 == 1))
    bx = send(b0, moves(0, 1, lambda k: k % 2 == 0))
    t2x = send(t2, swap)
    edgex = send(edge, moves(0, -1, lambda k: row_of(k) == 0 and k % 2 == 1))
    g_img, stats = call(
        k_late, [par], [stats], [b0, t2, edge, image, g_img], [f32, stat], [hbm, vmem],
        [block(3), block(), tails(), total], 14, 8, {6: 0},
    )
    grad_text = logit_params[0] * (g_txt + back.astype(jnp.float32))
    grad_text, t2x, edgex, bx = tie((grad_text, t2x, edgex, bx))
    g_img, stats = call(
        k_more, [par], [stats], [image, t2x, bx, edgex, g_img], [f32, stat], [hbm, vmem],
        [block(2), block(), tails(), total], 6, 0, {6: 0},
    )
    home, g_img = tie((home, g_img))
    grad_image, stats = call(
        k_tail, [par], [stats, home, g_img], [], [f32, jax.ShapeDtypeStruct((3, n), jnp.float32)], [vmem, vmem], [], 0, 0,
    )
    return grad_image, grad_text, stats


def solution(mesh):
    return jax.shard_map(
        on_device,
        mesh=mesh,
        in_specs=(P(AXES, None), P(AXES, None), P(AXES), P()),
        out_specs=(P(AXES, None), P(AXES, None), P(None, AXES)),
        check_vma=False,
    )
```

```python
import functools

import jax
import jax.numpy as jnp
from jax import lax
from jax.experimental import pallas as pl
from jax.experimental.pallas import tpu as pltpu
from jax.sharding import PartitionSpec as P

STEPS = 4
AXES = ("grp", "blk")
TAIL = 16


def dot_nt(a, b):
    return lax.dot_general(a, b, (((1,), (1,)), ((), ())), preferred_element_type=jnp.float32)


def dot_nn(a, b):
    return lax.dot_general(a, b, (((1,), (0,)), ((), ())), preferred_element_type=jnp.float32)


def dot_tn(a, b):
    return lax.dot_general(a, b, (((0,), (0,)), ((), ())), preferred_element_type=jnp.float32)


def spot(cycle):
    place = lax.axis_index("blk")
    return lax.rem(place, 2), lax.div(lax.rem(place, cycle // 2), 2), cycle // 4 - 1


def decode(tail, n):
    codes = tail[:, 0:n].astype(jnp.float32)
    return codes[0:1, :] * 64.0 + codes[1:2, :]


def pair(par, texts, images, rel, row, want_stats):
    scale, bias = par[0], par[1]
    raw = dot_nt(texts, images)
    z = scale * raw + bias
    pos = rel == row
    e = jnp.exp(-jnp.abs(z))
    part = 1.0 / (1.0 + e)
    sig = jnp.where(z >= 0.0, part, e * part)
    grad = jnp.where(pos, sig - 1.0, sig)
    low = grad.astype(jnp.bfloat16)
    if not want_stats:
        return low, None
    loss = jnp.maximum(jnp.where(pos, -z, z), 0.0) + jnp.log1p(e)
    sums = [jnp.sum(v, axis=0, keepdims=True) for v in (loss, grad, grad * raw)]
    return low, jnp.concatenate(sums, axis=0)


def rows(n, *bases):
    one = lax.broadcasted_iota(jnp.int32, (n, 1), 0)
    return jnp.concatenate([one + b for b in bases], axis=0).astype(jnp.float32)


def copy(source, target, sem):
    return pltpu.make_async_copy(source, target, sem)


def start(*copies):
    for c in copies:
        c.start()


def wait(*copies):
    for c in copies:
        c.wait()


def k_pack(label, image_h, text_h, full_h, other_h, out_h, image, text, code, sem, *, cycle, groups):
    core, row, _ = spot(cycle)
    n = image.shape[0]
    load_i, load_t = copy(image_h, image, sem.at[0]), copy(text_h, text, sem.at[1])
    start(load_i, load_t)
    here = label[...].reshape(1, n)
    owner = lax.div(here, n)
    rnd = lax.rem(lax.axis_index("grp") - lax.div(owner, cycle) + groups, groups)
    step = lax.rem(lax.axis_index("blk") - lax.rem(owner, cycle) + cycle, cycle)
    rel = rnd * (STEPS * n) + step * n + lax.rem(here, n)
    code[...] = jnp.zeros(code.shape, jnp.bfloat16)
    fill = jnp.zeros((TAIL - 2, n), jnp.float32)
    parts = [lax.div(rel, 64).astype(jnp.float32), lax.rem(rel, 64).astype(jnp.float32), fill]
    code[:, 0:n] = jnp.concatenate(parts, axis=0).astype(jnp.bfloat16)
    marks = [copy(code, t.at[n : n + TAIL], sem.at[q + 2]) for q, t in enumerate((full_h, other_h, out_h))]
    start(*marks)
    wait(load_i, load_t)
    whole = copy(image, full_h.at[0:n], sem.at[5])
    whole.start()

    @pl.when(core == 0)
    def _():
        copy(text, other_h.at[0:n], sem.at[6]).start()

    @pl.when(core == 1)
    def _():
        copy(image, other_h.at[0:n], sem.at[6]).start()

    @pl.when((core == 0) & (row == 1))
    def _():
        copy(image, out_h.at[0:n], sem.at[7]).start()

    @pl.when((core == 1) | (row != 1))
    def _():
        copy(text, out_h.at[0:n], sem.at[7]).start()

    wait(*marks, whole)
    copy(text, other_h.at[0:n], sem.at[6]).wait()
    copy(text, out_h.at[0:n], sem.at[7]).wait()


def k_mix(inner_h, text_h, out_h, hold, sem, *, cycle):
    _, row, last = spot(cycle)

    @pl.when(row != last)
    def _():
        copy(inner_h, hold, sem.at[0]).start()

    @pl.when(row == last)
    def _():
        copy(text_h, hold, sem.at[0]).start()

    copy(inner_h, hold, sem.at[0]).wait()
    out = copy(hold, out_h, sem.at[1])
    out.start()
    out.wait()


def k_first(par, image_h, text_h, other_h, gi_h, gt_h, st, image, tail, text, extra, etail, gi, gt, sem, *, cycle):
    core, _, _ = spot(cycle)
    n = text.shape[0]
    loads = [
        copy(image_h.at[0:n], image, sem.at[0]),
        copy(image_h.at[n : n + TAIL], tail, sem.at[1]),
        copy(text_h, text, sem.at[2]),
        copy(other_h.at[0:n], extra, sem.at[3]),
        copy(other_h.at[n : n + TAIL], etail, sem.at[4]),
    ]
    start(*loads)
    wait(*loads[0:3])
    rel = decode(tail[...], n)
    low, sums = pair(par, text[...], image[...], rel, rows(n, 0), True)
    gt[...] = dot_nn(low, image[...])
    gi[...] = dot_tn(low, text[...])
    st[0:3, :] = sums
    wait(*loads[3:])

    @pl.when(core == 1)
    def _():
        low, sums = pair(par, extra[...], image[...], rel, rows(n, n), True)
        gi[...] += dot_tn(low, extra[...])
        st[0:3, :] += sums

    @pl.when(core == 0)
    def _():
        low, _ = pair(par, text[...], extra[...], decode(etail[...], n), rows(n, n), False)
        gt[...] += dot_nn(low, extra[...])

    out = [copy(gi, gi_h, sem.at[5]), copy(gt, gt_h, sem.at[6])]
    start(*out)
    wait(*out)


def k_second(
    par, st0, image_h, text_h, t1_h, t1x_h, i1_h, i1x_h, gi0_h, gt0_h, gi_h, gt_h, st,
    image, tail, text, texts, images, tails, gi, gt, sem, *, cycle,
):
    core, row, _ = spot(cycle)
    n = text.shape[0]
    near = core == 0
    loads = [
        copy(image_h.at[0:n], image, sem.at[0]),
        copy(image_h.at[n : n + TAIL], tail, sem.at[1]),
        copy(gi0_h, gi, sem.at[4]),
    ]

    @pl.when((row > 0) | near)
    def _():
        copy(t1_h, texts.at[0:n], sem.at[2]).start()

    @pl.when((row == 0) & (core == 1))
    def _():
        copy(t1x_h, texts.at[0:n], sem.at[2]).start()

    @pl.when(row > 0)
    def _():
        copy(t1x_h, texts.at[n : 2 * n], sem.at[3]).start()

    more = [
        copy(text_h, text, sem.at[5]),
        copy(i1_h.at[0:n], images.at[0:n], sem.at[6]),
        copy(i1_h.at[n : n + TAIL], tails.at[0:TAIL], sem.at[7]),
        copy(i1x_h.at[0:n], images.at[n : 2 * n], sem.at[8]),
        copy(i1x_h.at[n : n + TAIL], tails.at[TAIL : 2 * TAIL], sem.at[9]),
        copy(gt0_h, gt, sem.at[10]),
    ]
    out_i = copy(gi, gi_h, sem.at[11])
    start(*loads, *more)
    wait(*loads)
    copy(t1_h, texts.at[0:n], sem.at[2]).wait()

    @pl.when(row > 0)
    def _():
        copy(t1x_h, texts.at[n : 2 * n], sem.at[3]).wait()
        row_i = rows(n, 2 * n, jnp.where(near, n, 3 * n))
        low, sums = pair(par, texts[...], image[...], decode(tail[...], n), row_i, True)
        gi[...] += dot_tn(low, texts[...])
        st[0:3, :] = st0[0:3, :] + sums

    @pl.when(row == 0)
    def _():
        row_i = rows(n, jnp.where(near, 2 * n, 3 * n))
        low, sums = pair(par, texts[0:n, :], image[...], decode(tail[...], n), row_i, True)
        gi[...] += dot_tn(low, texts[0:n, :])
        st[0:3, :] = st0[0:3, :] + sums

    out_i.start()
    wait(*more)
    rel = jnp.concatenate(
        [
            decode(tails[0:TAIL, :], n) - jnp.float32(2 * n),
            decode(tails[TAIL : 2 * TAIL, :], n) - jnp.where(near, 3 * n, n).astype(jnp.float32),
        ],
        axis=1,
    )
    low, _ = pair(par, text[...], images[...], rel, rows(n, 0), False)
    gt[...] += dot_nn(low, images[...])
    out_t = copy(gt, gt_h, sem.at[12])
    out_t.start()
    wait(out_i, out_t)


def k_cross(
    par, inner_h, out_h, image_h, other_h, i1_h, i1x_h, i2_h, iw_h, own_h, gt0_h, out, b0_h, gt_h,
    text, images, tails, own, gt, sem, *, cycle,
):
    core, row, last = spot(cycle)
    n = text.shape[0]
    near = core == 0

    def part(source, q):
        return (
            copy(source.at[0:n], images.at[q * n : (q + 1) * n], sem.at[2 * q]),
            copy(source.at[n : n + TAIL], tails.at[q * TAIL : (q + 1) * TAIL], sem.at[2 * q + 1]),
        )

    late = (row == 0) | ((row == last) & (core == 0))

    @pl.when(late)
    def _():
        copy(out_h, text, sem.at[8]).start()

    @pl.when(jnp.logical_not(late))
    def _():
        copy(inner_h, text, sem.at[8]).start()

    for q, source in enumerate((image_h, i1_h, i1x_h)):
        start(*part(source, q))

    @pl.when(near)
    def _():
        start(*part(other_h, 3))

    @pl.when((core == 1) & (row != last))
    def _():
        start(*part(i2_h, 3))

    @pl.when((core == 1) & (row == last))
    def _():
        start(*part(iw_h, 3))

    @pl.when((core == 1) & (row > 0))
    def _():
        start(copy(own_h, own, sem.at[10]), copy(gt0_h, gt, sem.at[11]))

    copy(inner_h, text, sem.at[8]).wait()
    keep = copy(text, b0_h, sem.at[9])
    keep.start()
    for q in range(4):
        wait(*part(image_h, q))
    steps = (0, 2 * n, jnp.where(near, 3 * n, n), jnp.where(near, n, 3 * n))
    rel = [
        decode(tails[q * TAIL : (q + 1) * TAIL, :], n) - jnp.asarray(s + STEPS * n, jnp.float32)
        for q, s in enumerate(steps)
    ]
    row_t = rows(n, 0)
    first, _ = pair(par, text[...], images[0 : 2 * n, :], jnp.concatenate(rel[0:2], axis=1), row_t, False)
    second, _ = pair(par, text[...], images[2 * n : 4 * n, :], jnp.concatenate(rel[2:4], axis=1), row_t, False)
    out[...] = dot_nn(jnp.concatenate([first, second], axis=1), images[...]).astype(jnp.bfloat16)

    @pl.when((core == 1) & (row > 0))
    def _():
        wait(copy(own_h, own, sem.at[10]), copy(gt0_h, gt, sem.at[11]))
        mine = decode(tails[3 * TAIL : 4 * TAIL, :], n)
        low, _ = pair(par, own[...], images[3 * n : 4 * n, :], mine, rows(n, 3 * n), False)
        gt[...] += dot_nn(low, images[3 * n : 4 * n, :])
        done = copy(gt, gt_h, sem.at[12])
        done.start()
        done.wait()

    keep.wait()


def k_away(
    par, image_h, t1_h, edge_h, early_h, over_h, mix_h, own_h, i2_h, gt0_h, out_h, t2_h, gt_h,
    image, tail, texts, out, own, extra, etail, gt, sem, *, cycle,
):
    core, row, _ = spot(cycle)
    n = t1_h.shape[0]
    first, second = texts.at[0:n], texts.at[n : 2 * n]

    @pl.when(row == 1)
    def _():
        copy(over_h, second, sem.at[0]).start()

    @pl.when((row == 0) & (core == 0))
    def _():
        copy(early_h, second, sem.at[0]).start()

    @pl.when((row > 1) | ((row == 0) & (core == 1)))
    def _():
        copy(mix_h, second, sem.at[0]).start()

    @pl.when(row == 0)
    def _():
        copy(edge_h.at[0:n], first, sem.at[3]).start()

    @pl.when(row != 0)
    def _():
        copy(t1_h, first, sem.at[3]).start()

    loads = [copy(image_h.at[0:n], image, sem.at[1]), copy(image_h.at[n : n + TAIL], tail, sem.at[2])]
    start(*loads)
    more = [
        copy(own_h, own, sem.at[6]),
        copy(i2_h.at[0:n], extra, sem.at[7]),
        copy(i2_h.at[n : n + TAIL], etail, sem.at[8]),
        copy(gt0_h, gt, sem.at[9]),
    ]

    @pl.when((core == 1) & (row == 0))
    def _():
        start(*more)

    copy(mix_h, second, sem.at[0]).wait()
    keep = copy(second, t2_h, sem.at[4])
    keep.start()
    copy(t1_h, first, sem.at[3]).wait()
    wait(*loads)

    @pl.when(core == 1)
    def _():
        row_i = rows(n, 3 * n, (STEPS + 3) * n)
        low, sums = pair(par, texts[...], image[...], decode(tail[...], n), row_i, True)
        out[0:n, :] = dot_tn(low, texts[...]).astype(jnp.bfloat16)
        high = sums.astype(jnp.bfloat16)
        rest = sums - high.astype(jnp.float32)
        mid = rest.astype(jnp.bfloat16)
        end = (rest - mid.astype(jnp.float32)).astype(jnp.bfloat16)
        fill = jnp.zeros((TAIL - 9, n), jnp.bfloat16)
        out[n : n + TAIL, :] = jnp.zeros((TAIL, out.shape[1]), jnp.bfloat16)
        out[n : n + TAIL, 0:n] = jnp.concatenate([high, mid, end, fill], axis=0)
        done = copy(out, out_h, sem.at[5])
        done.start()
        done.wait()

    @pl.when((core == 1) & (row == 0))
    def _():
        wait(*more)
        low, _ = pair(par, own[...], extra[...], decode(etail[...], n), rows(n, 3 * n), False)
        gt[...] += dot_nn(low, extra[...])
        back = copy(gt, gt_h, sem.at[10])
        back.start()
        back.wait()

    keep.wait()


def k_late(
    par, st0, b0_h, t2_h, edge_h, image_h, gi0_h, gi_h, st, texts, image, tail, gi, sem, *, cycle,
):
    core, row, _ = spot(cycle)
    n = image.shape[0]
    far = STEPS * n
    loads = [
        copy(b0_h, texts.at[0:n], sem.at[0]),
        copy(t2_h, texts.at[n : 2 * n], sem.at[1]),
        copy(image_h.at[0:n], image, sem.at[3]),
        copy(image_h.at[n : n + TAIL], tail, sem.at[4]),
        copy(gi0_h, gi, sem.at[5]),
    ]
    start(*loads)

    @pl.when((row == 0) & (core == 1))
    def _():
        copy(edge_h.at[0:n], texts.at[2 * n : 3 * n], sem.at[11]).start()

    wait(*loads[0:4])
    rel = decode(tail[...], n)

    @pl.when((row == 0) & (core == 1))
    def _():
        copy(edge_h.at[0:n], texts.at[2 * n : 3 * n], sem.at[11]).wait()
        low, sums = pair(par, texts[...], image[...], rel, rows(n, far, far + 2 * n, 2 * n), True)
        st[0:3, :] = st0[0:3, :] + sums
        loads[4].wait()
        gi[...] += dot_tn(low, texts[...])

    @pl.when((row != 0) | (core != 1))
    def _():
        low, sums = pair(par, texts[0 : 2 * n, :], image[...], rel, rows(n, far, far + 2 * n), True)
        st[0:3, :] = st0[0:3, :] + sums
        loads[4].wait()
        gi[...] += dot_tn(low, texts[0 : 2 * n, :])

    done = copy(gi, gi_h, sem.at[12])
    done.start()
    done.wait()


def k_more(par, st0, image_h, t2x_h, bx_h, edgex_h, gi0_h, gi_h, st, texts, image, tail, gi, sem, *, cycle):
    core, row, _ = spot(cycle)
    n = image.shape[0]
    far = STEPS * n
    loads = [
        copy(t2x_h, texts.at[0:n], sem.at[0]),
        copy(image_h.at[0:n], image, sem.at[1]),
        copy(image_h.at[n : n + TAIL], tail, sem.at[2]),
        copy(gi0_h, gi, sem.at[3]),
    ]
    start(*loads)

    @pl.when(core == 1)
    def _():
        copy(bx_h, texts.at[n : 2 * n], sem.at[4]).start()

    @pl.when((row == 0) & (core == 0))
    def _():
        copy(edgex_h.at[0:n], texts.at[n : 2 * n], sem.at[4]).start()

    wait(*loads[0:3])
    rel = decode(tail[...], n)
    two = (row == 0) | (core == 1)

    @pl.when(two)
    def _():
        copy(t2x_h, texts.at[n : 2 * n], sem.at[4]).wait()
        row_i = rows(n, far + jnp.where(core == 0, n, 3 * n), n + jnp.where(core == 0, 0, far))
        low, sums = pair(par, texts[...], image[...], rel, row_i, True)
        st[0:3, :] = st0[0:3, :] + sums
        loads[3].wait()
        gi[...] += dot_tn(low, texts[...])

    @pl.when(jnp.logical_not(two))
    def _():
        low, sums = pair(par, texts[0:n, :], image[...], rel, rows(n, far + n), True)
        st[0:3, :] = st0[0:3, :] + sums
        loads[3].wait()
        gi[...] += dot_tn(low, texts[0:n, :])

    done = copy(gi, gi_h, sem.at[5])
    done.start()
    done.wait()


def k_tail(par, st0, home, g0, gi, st, *, cycle):
    core, _, _ = spot(cycle)
    n, d = gi.shape

    @pl.when(core == 0)
    def _():
        gi[...] = par[0] * (g0[...] + home[0:n, :].astype(jnp.float32))
        parts = home[n : n + TAIL, 0:n].astype(jnp.float32)
        st[...] = st0[0:3, :] + parts[0:3] + parts[3:6] + parts[6:9]

    @pl.when(core == 1)
    def _():
        gi[...] = par[0] * g0[...]
        st[...] = st0[0:3, :]


def on_device(image_emb, text_emb, labels, logit_params):
    n, d = image_emb.shape
    groups = lax.axis_size("grp")
    cycle = lax.axis_size("blk")
    half = cycle // 2
    last = half // 2 - 1
    tie = lax.optimization_barrier

    def row_of(k):
        return k % half // 2

    def inner(k):
        return 0 < row_of(k) < last

    def send(value, pairs):
        return lax.ppermute(value, AXES, pairs)

    def moves(dg, dk, keep=lambda k: True):
        return [
            (g * cycle + k, (g + dg) % groups * cycle + (k + dk) % cycle)
            for g in range(groups)
            for k in range(cycle)
            if keep(k)
        ]

    swap = moves(0, 1, lambda k: k % 2 == 0) + moves(0, -1, lambda k: k % 2 == 1)

    par = logit_params
    f32 = jax.ShapeDtypeStruct((n, d), jnp.float32)
    low = jax.ShapeDtypeStruct((n, d), jnp.bfloat16)
    full = jax.ShapeDtypeStruct((n + TAIL, d), jnp.bfloat16)
    stat = jax.ShapeDtypeStruct((8, n), jnp.float32)
    smem = pl.BlockSpec(memory_space=pltpu.SMEM)
    vmem = pl.BlockSpec(memory_space=pltpu.VMEM)
    hbm = pl.BlockSpec(memory_space=pl.ANY)

    def block(parts=1):
        return pltpu.VMEM((parts * n, d), jnp.bfloat16)

    def tails(parts=1):
        return pltpu.VMEM((parts * TAIL, d), jnp.bfloat16)

    total = pltpu.VMEM((n, d), jnp.float32)

    def call(body, params, small, big, outs, out_specs, scratch, sems, units, alias=None):
        return pl.pallas_call(
            functools.partial(body, cycle=cycle),
            out_shape=outs,
            in_specs=[smem] * len(params) + [vmem] * len(small) + [hbm] * len(big),
            out_specs=out_specs,
            scratch_shapes=[*scratch, pltpu.SemaphoreType.DMA((sems,))] if sems else [],
            input_output_aliases=alias or {},
            compiler_params=pltpu.CompilerParams(vmem_limit_bytes=24 * 1024 * 1024),
            cost_estimate=pl.CostEstimate(flops=units, bytes_accessed=units, transcendentals=0),
        )(*params, *small, *big)

    def ahead(k):
        return row_of(k) == last and k % 2 == 0

    def behind(k):
        return row_of(k) == last and k % 2 == 1

    t1 = send(text_emb, moves(0, 2, lambda k: not behind(k)))
    b_in = send(text_emb, moves(1, 0, lambda k: inner(k) or behind(k)))
    early = send(text_emb, moves(1, 2, ahead))
    image, other, leaves = call(
        functools.partial(k_pack, groups=groups), [], [labels], [image_emb, text_emb], [full] * 3, [hbm] * 3,
        [block(), block(), tails()], 8, 0,
    )
    i1 = send(image, moves(0, -2))
    other = send(other, swap)
    g_img, g_txt, stats = call(
        k_first, [par], [], [image, text_emb, other], [f32, f32, stat], [hbm, hbm, vmem],
        [block(), tails(), block(), block(), tails(), total, total], 7, 5,
    )
    t1, i1, b_in, early, leaves, text, image, g_img = tie((t1, i1, b_in, early, leaves, text_emb, image, g_img))

    b_out = send(text, moves(1, 0, lambda k: row_of(k) == 0 or ahead(k)))
    mix = call(k_mix, [], [], [b_in, text], low, hbm, [block()], 2, 0)
    t2_mix = send(mix, moves(0, 2, inner) + moves(1, 2, behind))
    t2_over = send(t1, moves(1, 0, lambda k: row_of(k) == 1))
    t1x = send(t1, swap)
    i1x = send(i1, swap)
    i2 = send(i1, moves(0, -1, lambda k: k % 2 == 0 and k % half != 0))
    edge = send(leaves, moves(0, 2, behind) + moves(0, -3, lambda k: k % half == 2))
    g_img, g_txt, stats = call(
        k_second, [par], [stats], [image, text, t1, t1x, i1, i1x, g_img, g_txt], [f32, f32, stat], [hbm, hbm, vmem],
        [block(), tails(), block(), block(2), block(2), tails(2), total, total], 13, 8, {8: 0, 9: 1},
    )
    b_out, b_in, edge, t2_over, g_img, g_txt = tie((b_out, b_in, edge, t2_over, g_img, g_txt))
    cross, b0, g_txt = call(
        k_cross, [par], [], [b_in, b_out, image, other, i1, i1x, i2, edge, text, g_txt], [low, low, f32], [vmem, hbm, hbm],
        [block(), block(4), tails(4), block(), total], 13, 8, {10: 2},
    )
    back = send(cross, moves(-1, 0))
    t2_mix, t2_over, cross = tie((t2_mix, t2_over, cross))
    away, t2, g_txt = call(
        k_away, [par], [], [i1x, t1, edge, early, t2_over, t2_mix, text, i2, g_txt], [full, low, f32], [hbm] * 3,
        [block(), tails(), block(2), pltpu.VMEM((n + TAIL, d), jnp.bfloat16), block(), block(), tails(), total], 11, 4, {9: 2},
    )
    home = send(away, moves(0, 1, lambda k: k % 2 == 1))
    bx = send(b0, moves(0, 1, lambda k: k % 2 == 0))
    t2x = send(t2, swap)
    edgex = send(edge, moves(0, -1, lambda k: row_of(k) == 0 and k % 2 == 1))
    g_img, stats = call(
        k_late, [par], [stats], [b0, t2, edge, image, g_img], [f32, stat], [hbm, vmem],
        [block(3), block(), tails(), total], 14, 8, {6: 0},
    )
    grad_text = logit_params[0] * (g_txt + back.astype(jnp.float32))
    grad_text, t2x, edgex, bx = tie((grad_text, t2x, edgex, bx))
    g_img, stats = call(
        k_more, [par], [stats], [image, t2x, bx, edgex, g_img], [f32, stat], [hbm, vmem],
        [block(2), block(), tails(), total], 6, 0, {6: 0},
    )
    home, g_img = tie((home, g_img))
    grad_image, stats = call(
        k_tail, [par], [stats, home, g_img], [], [f32, jax.ShapeDtypeStruct((3, n), jnp.float32)], [vmem, vmem], [], 0, 0,
    )
    return grad_image, grad_text, stats


def solution(mesh):
    return jax.shard_map(
        on_device,
        mesh=mesh,
        in_specs=(P(AXES, None), P(AXES, None), P(AXES), P()),
        out_specs=(P(AXES, None), P(AXES, None), P(None, AXES)),
        check_vma=False,
    )
```
